256 devices in a mesh: dp: 16 (over z_lo, y), tensor: 16 (over z_hi, x, core).
Axes of the slice: x: 4, y: 4, z: 8 (z_hi: 2, z_lo: 4; z = z_hi * 4 + z_lo), core: 2. Of those that a mesh axis runs over, the one named last changes fastest.
Arguments:
- d_out: bfloat16 [2048, 8192], P('dp'), may hold values from -6 to 6
- gate_pre: bfloat16 [2048, 28672], P('dp', 'tensor'), may hold values from -6 to 6
- up_pre: bfloat16 [2048, 28672], P('dp', 'tensor'), may hold values from -6 to 6
- down_weight: bfloat16 [28672, 8192], P('tensor', 'dp'), may hold values from -0.03125 to 0.03125
- step_size: float32 [112, 8192], P('tensor', 'dp'), may hold values from 0.001 to 0.004
Outputs:
- d_gate: bfloat16 [2048, 28672], P('dp', 'tensor')
- d_up: bfloat16 [2048, 28672], P('dp', 'tensor')
- weight_grad: float32 [28672, 8192], P('tensor', 'dp')
- step_grad: float32 [112, 8192], P('tensor', 'dp')
The draws below stay inside these ranges and needn't reach their ends.
All inputs are finite; a program needn't handle non-finite values.
Results may differ from the reference program's by a relative error of at most 0.025.
Values may be sent and summed in bfloat16 or wider, within the bound.
A program may use at most 128 MiB of HBM per device.

```python
import math
import jax
import jax.numpy as jnp
import numpy as np
from jax import lax

D = 8192
FF = 28672
GROUP = 256
TOKENS = 2048


def shard_levels(key, dims, shards, least, top_value):
    def one(axis_at, blocks):
        heights = jax.random.uniform(jax.random.fold_in(jax.random.fold_in(key, 6), axis_at), (blocks,), jnp.float32, least / len(shards), top_value / len(shards))
        return jnp.repeat(jnp.exp(heights), dims[axis_at] // blocks).reshape((-1,) + (1,) * (len(dims) - axis_at - 1))

    gain = one(*shards[0])
    for cut in shards[1:]:
        gain = gain * one(*cut)
    return gain


def scatter_about(rng, dims, spread, bound, pieces=(), held_as=jnp.bfloat16):
    result = jax.random.normal(rng, dims, jnp.float32) * spread
    if len(pieces) > 0:
        result = shard_levels(rng, dims, pieces, -0.22, 0.18) * result
    return jnp.clip(result, min=-bound, max=bound).astype(held_as)


def setup_inputs(seed: int = 0) -> dict:
    splits = jax.random.split(jax.random.key(seed), 6)
    d_out = scatter_about(splits[0], (TOKENS, D), 1.0, 6.0, ((0, 16),))
    gate_pre = scatter_about(splits[1], (TOKENS, FF), 1.0, 6.0, ((0, 16), (1, 16)))
    up_pre = scatter_about(splits[2], (TOKENS, FF), 1.0, 6.0, ((0, 16), (1, 16)))
    down_weight = scatter_about(splits[3], (FF, D), FF ** -0.5, 0.03125, ((0, 16), (1, 16)))
    step_size = jnp.clip(jnp.exp(math.log(0.004) - 1.3862944 * jax.random.uniform(splits[4], (FF // GROUP, D), jnp.float32) ** shard_levels(splits[4], (FF // GROUP, D), ((0, 16), (1, 16)), -0.2, 0.2)), 0.001, 0.004)
    return {"d_out": d_out, "gate_pre": gate_pre, "up_pre": up_pre, "down_weight": down_weight, "step_size": step_size}


def paley_matrix():
    digits_of = [(number % 3, number // 3 % 3, number // 9) for number in range(27)]
    lookup = {digits: number for number, digits in enumerate(digits_of)}

    def field_product(left_poly, right_poly):
        coeffs = [0, 0, 0, 0, 0]
        for left_pos in range(3):
            for right_pos in range(3):
                coeffs[left_pos + right_pos] += left_poly[left_pos] * right_poly[right_pos]
        for degree in (4, 3):
            excess = coeffs[degree]
            coeffs[degree] = 0
            coeffs[degree - 2] += excess
            coeffs[degree - 3] += 2 * excess
        return tuple((coefficient % 3 for coefficient in coeffs[:3]))
    squares_set = set((lookup[field_product(digits, digits)] for digits in digits_of[1:]))
    matrix_out = np.eye(28, dtype=np.float32)
    matrix_out[0, 1:] += 1.0
    matrix_out[1:, 0] -= 1.0
    for row_num in range(27):
        for col_num in range(27):
            if row_num != col_num:
                diff_poly = tuple(((digits_of[row_num][position] - digits_of[col_num][position]) % 3 for position in range(3)))
                matrix_out[row_num + 1, col_num + 1] += 1.0 if lookup[diff_poly] in squares_set else -1.0
    return matrix_out

def sylvester(order_size):
    indices = np.arange(order_size)
    anded = indices[:, None] & indices[None, :]
    parity = np.zeros((order_size, order_size), np.int64)
    for bit_num in range(int(order_size).bit_length()):
        parity = parity + (anded >> bit_num & 1)
    return (1 - 2 * (parity % 2)).astype(np.float32)

def rotate_rows(tok_block, paley_table, sylvester_table, backward):
    count_rows = tok_block.shape[0]
    block_width = sylvester_table.shape[0]
    mixed_rows = jnp.dot(tok_block.reshape(count_rows * 28, block_width), jnp.asarray(sylvester_table, jnp.bfloat16), preferred_element_type=jnp.float32)
    coupling = paley_table.T if backward else paley_table
    mixed_rows = jnp.einsum('tab,ac->tcb', mixed_rows.reshape(count_rows, 28, block_width), jnp.asarray(coupling, jnp.float32), precision=lax.Precision.HIGHEST)
    return (mixed_rows.reshape(count_rows, 28 * block_width) * (1.0 / math.sqrt(28 * block_width))).astype(jnp.bfloat16)

def fake_quantize(weights_block, step_block):
    group_count = step_block.shape[0]
    shaped = weights_block.astype(jnp.float32).reshape(group_count, weights_block.shape[0] // group_count, weights_block.shape[1])
    ratios = shaped / step_block[:, None, :]
    clipped = jnp.clip(ratios, -8.0, 7.0)
    turned = 2.0 * math.pi * clipped
    levels = clipped - jnp.sin(turned) / (2.0 * math.pi)
    slopes = 1.0 - jnp.cos(turned)
    quantized = (step_block[:, None, :] * levels).reshape(weights_block.shape).astype(jnp.bfloat16)
    return (quantized, ratios, levels, slopes)

def gradients_from(d_quant, ratios, levels, slopes):
    shaped = d_quant.reshape(ratios.shape)
    weight_grad = (shaped * slopes).reshape(d_quant.shape)
    step_grad = lax.optimization_barrier(jnp.sum(shaped * (levels - ratios * slopes), axis=1)) * (1.0 / math.sqrt(7.0 * ratios.shape[1]))
    return (weight_grad, step_grad)

def reference(d_out, gate_pre, up_pre, down_weight, step_size):
    gate_wide = gate_pre.astype(jnp.float32)
    up_wide = up_pre.astype(jnp.float32)
    sig = jax.nn.sigmoid(gate_wide)
    hidden = (gate_wide * sig * up_wide).astype(jnp.bfloat16)
    paley_table = paley_matrix()
    sylvester_table = sylvester(FF // 28)
    h_rot = rotate_rows(hidden, paley_table, sylvester_table, False)
    quantized, ratios, levels, slopes = fake_quantize(down_weight, step_size)
    grad_rot = lax.dot_general(d_out, quantized, (((1,), (1,)), ((), ())), preferred_element_type=jnp.float32).astype(jnp.bfloat16)
    grad_hidden = rotate_rows(grad_rot, paley_table, sylvester_table, True).astype(jnp.float32)
    d_quant = lax.dot_general(h_rot, d_out, (((0,), (0,)), ((), ())), preferred_element_type=jnp.float32)
    weight_grad, step_grad = gradients_from(d_quant, ratios, levels, slopes)
    d_up = (grad_hidden * gate_wide * sig).astype(jnp.bfloat16)
    d_gate = (grad_hidden * up_wide * sig * (1.0 + gate_wide * (1.0 - sig))).astype(jnp.bfloat16)
    return (d_gate, d_up, weight_grad, step_grad)
```

```python
import functools
import math

import jax
import jax.numpy as jnp
import numpy as np
from jax import lax
from jax.experimental import pallas as pl
from jax.experimental.pallas import tpu as pltpu
from jax.sharding import PartitionSpec as P

FF = 28672
F32, BF16 = jnp.float32, jnp.bfloat16
MESH = pl.DeviceIdType.MESH
SCALE = 1.0 / math.sqrt(FF)


def paley_matrix():
    digits_of = [(number % 3, number // 3 % 3, number // 9) for number in range(27)]
    lookup = {digits: number for number, digits in enumerate(digits_of)}

    def field_product(left_poly, right_poly):
        coeffs = [0, 0, 0, 0, 0]
        for left_pos in range(3):
            for right_pos in range(3):
                coeffs[left_pos + right_pos] += left_poly[left_pos] * right_poly[right_pos]
        for degree in (4, 3):
            excess = coeffs[degree]
            coeffs[degree] = 0
            coeffs[degree - 2] += excess
            coeffs[degree - 3] += 2 * excess
        return tuple((coefficient % 3 for coefficient in coeffs[:3]))

    squares_set = set((lookup[field_product(digits, digits)] for digits in digits_of[1:]))
    matrix_out = np.eye(28, dtype=np.float32)
    matrix_out[0, 1:] += 1.0
    matrix_out[1:, 0] -= 1.0
    for row_num in range(27):
        for col_num in range(27):
            if row_num != col_num:
                diff_poly = tuple(
                    (
                        (digits_of[row_num][position] - digits_of[col_num][position]) % 3
                        for position in range(3)
                    )
                )
                matrix_out[row_num + 1, col_num + 1] += (
                    1.0 if lookup[diff_poly] in squares_set else -1.0
                )
    return matrix_out


def sylvester(order_size):
    indices = np.arange(order_size)
    anded = indices[:, None] & indices[None, :]
    parity = np.zeros((order_size, order_size), np.int64)
    for bit_num in range(int(order_size).bit_length()):
        parity = parity + (anded >> bit_num & 1)
    return (1 - 2 * (parity % 2)).astype(np.float32)


def half_turn_series():
    points = 0.125 - 0.125 * np.cos((np.arange(64) + 0.5) * np.pi / 64)
    root = np.sqrt(points)
    a = np.polyfit(points, np.sin(np.pi * root) / root, 5)
    b = np.polyfit(points, np.cos(np.pi * root), 6)
    return [float(v) for v in a], [float(v) for v in b]


def horner(coefficients, u):
    total = coefficients[0] * u + coefficients[1]
    for c in coefficients[2:]:
        total = total * u + c
    return total


def dot(a, b, ca, cb):
    return lax.dot_general(a, b, (((ca,), (cb,)), ((), ())), preferred_element_type=F32)


def mix_paley(paley, src, dst, scale):
    def step(b, carry):
        for half in range(2):
            rows = slice(8 * half, 8 * half + 8)
            x = [src[b, a, rows, :] for a in range(28)]
            whole = x
            while len(whole) > 1:
                whole = [whole[i] + whole[i + 1] if i + 1 < len(whole) else whole[i] for i in range(0, len(whole), 2)]
            for c in range(28):
                negative = [x[a] for a in range(28) if paley[a, c] < 0]
                if negative:
                    less = negative[0]
                    for n in negative[1:]:
                        less = less + n
                    src[4 + b, c, rows, :] = (whole[0] - 2.0 * less) * scale
                else:
                    src[4 + b, c, rows, :] = whole[0] * scale
        for c in range(28):
            dst[c * 4 + b] = src[4 + b, c].astype(BF16)
        return carry

    lax.fori_loop(0, 4, step, 0)


def kernel(
    dy_ref, gate_ref, up_ref, dw_ref, step_ref, h256_ref,
    dgate_ref, dup_ref, wg_ref, sg_ref,
    hid, hs, h1, mixf, h2, hb, dyb, qb, slopes, extra, gsend, gx, gsum, gr, gm, fr, gh, dsend, dx,
    s_loc, s_h1s, s_h1r, s_h2s, s_h2r, s_hxs, s_hxr, s_d1s, s_d1r, s_d2s, s_d2r, s_qs, s_qr,
    s_gxs, s_gxr, s_grs, s_grr, s_fs, s_fr, s_xs, s_xr,
):
    paley = paley_matrix()
    sin_series, cos_series = half_turn_series()
    d, t = lax.axis_index("dp"), lax.axis_index("tensor")
    z, y = d // 4, d % 4
    yi = y % 2
    yo = 1 - yi
    d_t = z * 4 + y + 1 - 2 * yi
    d_c = z * 4 + 3 - y
    di = y // 2
    do = 1 - di
    tg, lh = t // 2, t % 2
    part = t % 8
    hi8 = t - part

    def remote(src, dst, ss, rs, dev_d, dev_t):
        return pltpu.make_async_remote_copy(
            src_ref=src, dst_ref=dst, send_sem=ss, recv_sem=rs, device_id=(dev_d, dev_t), device_id_type=MESH
        )

    def await_bytes(ref, sem):
        pltpu.make_async_copy(ref, ref, sem).wait()

    def rows16(i):
        return pl.ds(pl.multiple_of(i * 16, 16), 16)

    def peer64(j):
        return lax.rem(z + j % 4, 4) , lax.rem(t + j // 4, 16)

    barrier = pltpu.get_barrier_semaphore()

    def greet(j, carry):
        zz, tt = peer64(j)
        pl.semaphore_signal(barrier, inc=1, device_id=(zz * 4 + y, tt), device_id_type=MESH)
        return carry

    lax.fori_loop(1, 64, greet, 0)
    for zz in range(4):
        pl.semaphore_signal(barrier, inc=1, device_id=(zz * 4 + y + 1 - 2 * yi, t), device_id_type=MESH)
    pl.semaphore_signal(barrier, inc=1, device_id=(d_c, t), device_id_type=MESH)

    def hidden_step(i, carry):
        rows = rows16(i)
        for q in range(7):
            cols = slice(256 * q, 256 * q + 256)
            g = gate_ref[rows, cols].astype(F32)
            u = up_ref[rows, cols].astype(F32)
            hid[rows, cols] = (g * jax.nn.sigmoid(g) * u).astype(BF16)
        return carry

    lax.fori_loop(0, 8, hidden_step, 0)
    for q in range(7):
        turned = dot(hid[:, 256 * q : 256 * q + 256], h256_ref[...], 1, 0).astype(BF16)
        hs[0, q] = turned[:, :128]
        hs[1, q] = turned[:, 128:]

    pl.semaphore_wait(barrier, 68)

    def send_h1(k, carry):
        p = lax.rem(t + k, 16)
        remote(hs.at[p % 2, :, rows16(p // 2), :], h1.at[pl.ds(7 * t, 7)], s_h1s, s_h1r, d, p).start()
        return carry

    pltpu.make_async_copy(hs.at[lh, :, rows16(tg), :], h1.at[pl.ds(7 * t, 7)], s_h1r).start()
    lax.fori_loop(1, 16, send_h1, 0)

    def columns(zz, yy, c):
        low = yy - (yy // 2) * (2 * yy - 3)
        return pl.ds(pl.multiple_of(512 * (zz * 4 + low + c * (3 - 2 * low)), 512), 512)

    def send_d1(j, carry):
        zz = lax.rem(z + j // 2, 4)
        yy = y - yi + lax.rem(yi + j % 2, 2)
        for c in range(2):
            remote(
                dy_ref.at[rows16(part), columns(zz, yy, c)],
                dyb.at[yi, z, rows16(part), pl.ds(512 * c, 512)],
                s_d1s, s_d1r, zz * 4 + yy, t,
            ).start()
        return carry

    for c in range(2):
        pltpu.make_async_copy(
            dy_ref.at[rows16(part), columns(z, y, c)], dyb.at[yi, z, rows16(part), pl.ds(512 * c, 512)], s_d1r
        ).start()
    lax.fori_loop(1, 8, send_d1, 0)

    def quant_group(g, carry):
        step = step_ref[pl.ds(g, 1), :]
        inverse = 1.0 / step

        def chunk(i, inner):
            rows = rows16(g * 16 + i)
            ratios = dw_ref[rows, :].astype(F32) * inverse
            clipped = jnp.clip(ratios, -8.0, 7.0)
            r = clipped - jnp.round(clipped)
            u = r * r
            s = r * horner(sin_series, u)
            c = horner(cos_series, u)
            levels = clipped - s * c * (1.0 / math.pi)
            slope = 2.0 * s * s
            slopes[rows, :] = slope
            extra[rows, :] = levels - ratios * slope
            qb[di, g, rows16(i), :] = (step * levels).astype(BF16)
            return inner

        lax.fori_loop(0, 16, chunk, 0)
        remote(qb.at[di, g], qb.at[di, g], s_qs.at[g], s_qr.at[g], d_c, t).start()
        return carry

    lax.fori_loop(0, 7, quant_group, 0)

    await_bytes(dyb.at[0, :, 0:32, :], s_d1r)

    def send_d2(k, carry):
        p = hi8 + lax.rem(part + k, 8)
        block = dyb.at[:, :, rows16(part), :]
        remote(block, block, s_d2s, s_d2r, d, p).start()
        return carry

    lax.fori_loop(1, 8, send_d2, 0)

    await_bytes(h1, s_h1r)

    def spread_h(a, carry):
        x = [h1[a * 4 + b].astype(F32) for b in range(4)]
        p0, p1, m0, m1 = x[0] + x[1], x[2] + x[3], x[0] - x[1], x[2] - x[3]
        mixf[0, a] = p0 + p1
        mixf[1, a] = m0 + m1
        mixf[2, a] = p0 - p1
        mixf[3, a] = m0 - m1
        return carry

    lax.fori_loop(0, 28, spread_h, 0)
    mix_paley(paley, mixf, h2, SCALE)

    def h_place(zz, ti):
        return hb.at[yi, ti % 2, :, pl.ds(pl.multiple_of(zz * 128 + (ti // 2) * 16, 16), 16), :]

    def send_h2(j, carry):
        zz, tt = peer64(j)
        remote(h2.at[pl.ds(7 * tt, 7)], h_place(z, t), s_h2s, s_h2r.at[z], zz * 4 + y, tt).start()
        return carry

    pltpu.make_async_copy(h2.at[pl.ds(7 * t, 7)], h_place(z, t), s_h2r.at[z]).start()
    lax.fori_loop(1, 64, send_h2, 0)

    await_bytes(dyb.at[:, :, 0:112, :], s_d2r)

    def product_g(which, g):
        total = dot(dyb[which, :, :, :512].reshape(512, 512), qb[0, g], 1, 1)
        return total + dot(dyb[which, :, :, 512:].reshape(512, 512), qb[1, g], 1, 1)

    def grad_group(g, carry):
        remote(qb.at[di, g], qb.at[do, g], s_qs.at[g], s_qr.at[g], d_c, t).wait_recv()
        theirs = product_g(yo, g).astype(BF16)
        gsend[g, 0] = theirs[:, :128]
        gsend[g, 1] = theirs[:, 128:]
        remote(gsend.at[g], gx.at[g], s_gxs.at[g], s_gxr.at[g], d_t, t).start()
        ours = product_g(yi, g).astype(BF16)
        gsum[0, g] = ours[:, :128]
        gsum[1, g] = ours[:, 128:]
        return carry

    lax.fori_loop(0, 7, grad_group, 0)

    def add_group(g, carry):
        remote(gsend.at[g], gx.at[g], s_gxs.at[g], s_gxr.at[g], d_t, t).wait_recv()

        def chunk(i, inner):
            rows = pl.ds(pl.multiple_of(i * 64, 64), 64)
            for k in range(2):
                gsum[k, g, rows, :] = (gsum[k, g, rows, :].astype(F32) + gx[g, k, rows, :].astype(F32)).astype(BF16)
            return inner

        return lax.fori_loop(0, 8, chunk, carry)

    lax.fori_loop(0, 7, add_group, 0)

    def g_piece(zz, ti):
        return gsum.at[ti % 2, :, pl.ds(pl.multiple_of(zz * 128 + (ti // 2) * 16, 16), 16), :]

    def g_place(zz, ti):
        return gr.at[pl.ds(zz * 112 + 7 * ti, 7)]

    def send_gr(j, carry):
        zz, tt = peer64(j)
        remote(g_piece(zz, tt), g_place(z, t), s_grs, s_grr, zz * 4 + y, tt).start()
        return carry

    pltpu.make_async_copy(g_piece(z, t), g_place(z, t), s_grr).start()
    lax.fori_loop(1, 64, send_gr, 0)

    def h_block(which, zz):
        return hb.at[which, :, :, pl.ds(pl.multiple_of(zz * 128, 128), 128), :]

    def forward_h(k, carry):
        zz = lax.rem(z + k, 4)
        await_bytes(h_block(yi, zz), s_h2r.at[zz])
        remote(h_block(yi, zz), h_block(yi, zz), s_hxs.at[k], s_hxr.at[k], d_t, t).start()
        return carry

    lax.fori_loop(0, 4, forward_h, 0)

    def receive_h(k, carry):
        zz = lax.rem(z + k, 4)
        remote(h_block(yi, zz), h_block(yo, zz), s_hxs.at[k], s_hxr.at[k], d_t, t).wait_recv()
        return carry

    lax.fori_loop(0, 4, receive_h, 0)

    def product_d(q, half, c):
        cols = pl.ds(pl.multiple_of(c * 512, 512), 512)
        total = dot(hb[0, half, q], dyb[0, :, :, cols].reshape(512, 512), 0, 0)
        return total + dot(hb[1, half, q], dyb[1, :, :, cols].reshape(512, 512), 0, 0)

    def weight_group(q, carry):
        for half in range(2):
            dsend[q, 128 * half : 128 * half + 128, :] = product_d(q, half, do).astype(BF16)
        remote(dsend.at[q], dx.at[q], s_xs.at[q], s_xr.at[q], d_c, t).start()
        for half in range(2):
            wg_ref[pl.ds(pl.multiple_of(q * 256 + 128 * half, 128), 128), :] = product_d(q, half, di)
        return carry

    lax.fori_loop(0, 7, weight_group, 0)

    await_bytes(gr, s_grr)

    def spread_g(a, carry):
        x = []
        for b in range(4):
            total = gr[a * 4 + b].astype(F32)
            for zz in range(1, 4):
                total = total + gr[112 * zz + a * 4 + b].astype(F32)
            x.append(total)
        p0, p1, m0, m1 = x[0] + x[1], x[2] + x[3], x[0] - x[1], x[2] - x[3]
        mixf[0, a] = p0 + p1
        mixf[1, a] = m0 + m1
        mixf[2, a] = p0 - p1
        mixf[3, a] = m0 - m1
        return carry

    lax.fori_loop(0, 28, spread_g, 0)
    mix_paley(paley.T, mixf, gm, SCALE)

    def f_place(ti):
        return fr.at[ti % 2, :, rows16(ti // 2), :]

    def send_f(k, carry):
        p = lax.rem(t + k, 16)
        remote(gm.at[pl.ds(7 * p, 7)], f_place(t), s_fs, s_fr, d, p).start()
        return carry

    pltpu.make_async_copy(gm.at[pl.ds(7 * t, 7)], f_place(t), s_fr).start()
    lax.fori_loop(1, 16, send_f, 0)
    await_bytes(fr, s_fr)

    for q in range(7):
        gh[...] = dot(fr[0, q], h256_ref[:128, :], 1, 0) + dot(fr[1, q], h256_ref[128:, :], 1, 0)
        cols = slice(256 * q, 256 * q + 256)

        def finish(i, carry, cols=cols):
            rows = rows16(i)
            g = gate_ref[rows, cols].astype(F32)
            u = up_ref[rows, cols].astype(F32)
            sig = jax.nn.sigmoid(g)
            grad = gh[rows, :] * sig
            dup_ref[rows, cols] = (grad * g).astype(BF16)
            dgate_ref[rows, cols] = (grad * u * (1.0 + g * (1.0 - sig))).astype(BF16)
            return carry

        lax.fori_loop(0, 8, finish, 0)

    def weight_finish(q, carry):
        remote(dsend.at[q], dx.at[q], s_xs.at[q], s_xr.at[q], d_c, t).wait_recv()

        def chunk(i, acc):
            rows = rows16(q * 16 + i)
            total = wg_ref[rows, :] + dx[q, rows16(i), :].astype(F32)
            wg_ref[rows, :] = total * slopes[rows, :]
            return acc + total * extra[rows, :]

        acc = lax.fori_loop(0, 16, chunk, jnp.zeros((16, 512), F32))
        sg_ref[pl.ds(q, 1), :] = jnp.sum(acc, axis=0, keepdims=True) * (1.0 / math.sqrt(1792.0))
        return carry

    lax.fori_loop(0, 7, weight_finish, 0)

    await_bytes(h1.at[0:105], s_h1s)
    await_bytes(gr.at[0:441], s_h2s)
    await_bytes(gr.at[0:441], s_grs)
    await_bytes(gm.at[0:105], s_fs)
    await_bytes(dyb.at[0, 0, 0:112, :], s_d1s)
    await_bytes(dyb.at[:, :, 0:112, :], s_d2s)

    def drain7(g, carry):
        remote(qb.at[di, g], qb.at[di, g], s_qs.at[g], s_qr.at[g], d_c, t).wait_send()
        remote(gsend.at[g], gx.at[g], s_gxs.at[g], s_gxr.at[g], d_t, t).wait_send()
        remote(dsend.at[g], dx.at[g], s_xs.at[g], s_xr.at[g], d_c, t).wait_send()
        return carry

    lax.fori_loop(0, 7, drain7, 0)

    def drain4(k, carry):
        zz = lax.rem(z + k, 4)
        remote(h_block(yi, zz), h_block(yi, zz), s_hxs.at[k], s_hxr.at[k], d_t, t).wait_send()
        return carry

    lax.fori_loop(0, 4, drain4, 0)


def shards(d_out, gate_pre, up_pre, down_weight, step_size):
    h256 = jnp.asarray(sylvester(256), BF16)
    vmem = pl.BlockSpec(memory_space=pltpu.VMEM)
    dma = pltpu.SemaphoreType.DMA
    return pl.pallas_call(
        kernel,
        out_shape=(
            jax.ShapeDtypeStruct((128, 1792), BF16),
            jax.ShapeDtypeStruct((128, 1792), BF16),
            jax.ShapeDtypeStruct((1792, 512), F32),
            jax.ShapeDtypeStruct((7, 512), F32),
        ),
        in_specs=[pl.BlockSpec(memory_space=pl.ANY)] + [vmem] * 5,
        out_specs=(vmem,) * 4,
        scratch_shapes=[
            pltpu.VMEM((128, 1792), BF16),
            pltpu.VMEM((2, 7, 128, 128), BF16),
            pltpu.VMEM((112, 16, 128), BF16),
            pltpu.VMEM((8, 28, 16, 128), F32),
            pltpu.VMEM((112, 16, 128), BF16),
            pltpu.VMEM((2, 2, 7, 512, 128), BF16),
            pltpu.VMEM((2, 4, 128, 1024), BF16),
            pltpu.VMEM((2, 7, 256, 512), BF16),
            pltpu.VMEM((1792, 512), F32),
            pltpu.VMEM((1792, 512), F32),
            pltpu.VMEM((7, 2, 512, 128), BF16),
            pltpu.VMEM((7, 2, 512, 128), BF16),
            pltpu.VMEM((2, 7, 512, 128), BF16),
            pltpu.VMEM((448, 16, 128), BF16),
            pltpu.VMEM((112, 16, 128), BF16),
            pltpu.VMEM((2, 7, 128, 128), BF16),
            pltpu.VMEM((128, 256), F32),
            pltpu.VMEM((7, 256, 512), BF16),
            pltpu.VMEM((7, 256, 512), BF16),
            dma,
            dma, dma,
            dma, dma((4,)),
            dma((4,)), dma((4,)),
            dma, dma,
            dma, dma,
            dma((7,)), dma((7,)),
            dma((7,)), dma((7,)),
            dma, dma,
            dma, dma,
            dma((7,)), dma((7,)),
        ],
        compiler_params=pltpu.CompilerParams(
            collective_id=0, has_side_effects=True, vmem_limit_bytes=58 * 1024 * 1024
        ),
        cost_estimate=pl.CostEstimate(flops=8_000_000_000, bytes_accessed=12_000_000, transcendentals=1_000_000),
    )(d_out, gate_pre, up_pre, down_weight, step_size, h256)


def solution(mesh):
    return jax.shard_map(
        shards,
        mesh=mesh,
        in_specs=(
            P("dp", None),
            P("dp", "tensor"),
            P("dp", "tensor"),
            P("tensor", "dp"),
            P("tensor", "dp"),
        ),
        out_specs=(P("dp", "tensor"), P("dp", "tensor"), P("tensor", "dp"), P("tensor", "dp")),
        check_vma=False,
    )
```

```python
import math

import jax
import jax.numpy as jnp
import numpy as np
from jax import lax
from jax.experimental import pallas as pl
from jax.experimental.pallas import tpu as pltpu
from jax.sharding import PartitionSpec as P

FF = 28672
F32, BF16 = jnp.float32, jnp.bfloat16
MESH = pl.DeviceIdType.MESH
SCALE = 1.0 / math.sqrt(FF)
CHUNKS = ((0, 4), (4, 3))


def paley_matrix():
    digits_of = [(number % 3, number // 3 % 3, number // 9) for number in range(27)]
    lookup = {digits: number for number, digits in enumerate(digits_of)}

    def field_product(left_poly, right_poly):
        coeffs = [0, 0, 0, 0, 0]
        for left_pos in range(3):
            for right_pos in range(3):
                coeffs[left_pos + right_pos] += left_poly[left_pos] * right_poly[right_pos]
        for degree in (4, 3):
            excess = coeffs[degree]
            coeffs[degree] = 0
            coeffs[degree - 2] += excess
            coeffs[degree - 3] += 2 * excess
        return tuple((coefficient % 3 for coefficient in coeffs[:3]))

    squares_set = set((lookup[field_product(digits, digits)] for digits in digits_of[1:]))
    matrix_out = np.eye(28, dtype=np.float32)
    matrix_out[0, 1:] += 1.0
    matrix_out[1:, 0] -= 1.0
    for row_num in range(27):
        for col_num in range(27):
            if row_num != col_num:
                diff_poly = tuple(
                    (
                        (digits_of[row_num][position] - digits_of[col_num][position]) % 3
                        for position in range(3)
                    )
                )
                matrix_out[row_num + 1, col_num + 1] += (
                    1.0 if lookup[diff_poly] in squares_set else -1.0
                )
    return matrix_out


def sylvester(order_size):
    indices = np.arange(order_size)
    anded = indices[:, None] & indices[None, :]
    parity = np.zeros((order_size, order_size), np.int64)
    for bit_num in range(int(order_size).bit_length()):
        parity = parity + (anded >> bit_num & 1)
    return (1 - 2 * (parity % 2)).astype(np.float32)


def half_turn_series():
    points = 0.125 - 0.125 * np.cos((np.arange(64) + 0.5) * np.pi / 64)
    root = np.sqrt(points)
    a = np.polyfit(points, np.sin(np.pi * root) / root, 5)
    b = np.polyfit(points, np.cos(np.pi * root), 6)
    return [float(v) for v in a], [float(v) for v in b]


def horner(coefficients, u):
    total = coefficients[0] * u + coefficients[1]
    for c in coefficients[2:]:
        total = total * u + c
    return total


def dot(a, b, ca, cb):
    return lax.dot_general(a, b, (((ca,), (cb,)), ((), ())), preferred_element_type=F32)


def mix_paley(paley, src, dst, scale):
    def step(b, carry):
        for half in range(2):
            rows = slice(8 * half, 8 * half + 8)
            x = [src[b, a, rows, :] for a in range(28)]
            whole = x
            while len(whole) > 1:
                whole = [whole[i] + whole[i + 1] if i + 1 < len(whole) else whole[i] for i in range(0, len(whole), 2)]
            for c in range(28):
                negative = [x[a] for a in range(28) if paley[a, c] < 0]
                if negative:
                    less = negative[0]
                    for n in negative[1:]:
                        less = less + n
                    src[4 + b, c, rows, :] = (whole[0] - 2.0 * less) * scale
                else:
                    src[4 + b, c, rows, :] = whole[0] * scale
        for c in range(28):
            dst[c * 4 + b] = src[4 + b, c].astype(BF16)
        return carry

    lax.fori_loop(0, 4, step, 0)


def kernel(
    dy_ref, gate_ref, up_ref, dw_ref, step_ref, h256_ref,
    fr, wg_ref, sg_ref,
    hid, hs, h1, mixf, h2, hb, dyb, qb, slopes, extra, gsend, gx, gsum, gr, gm, dsend, dx,
    s_h1s, s_h1r, s_h2s, s_h2r, s_hxs, s_hxr, s_d1s, s_d1r, s_d2s, s_d2r, s_d3s, s_d3r, s_qs, s_qr,
    s_gxs, s_gxr, s_grs, s_grr, s_fs, s_fr, s_xs, s_xr,
):
    paley = paley_matrix()
    sin_series, cos_series = half_turn_series()
    d, t = lax.axis_index("dp"), lax.axis_index("tensor")
    z, y = d // 4, d % 4
    yi = y % 2
    yo = 1 - yi
    d_t = z * 4 + y + 1 - 2 * yi
    d_c = z * 4 + 3 - y
    di = y // 2
    do = 1 - di
    tg, lh = t // 2, t % 2
    part = t % 8
    hi8 = t - part

    def remote(src, dst, ss, rs, dev_d, dev_t):
        return pltpu.make_async_remote_copy(
            src_ref=src, dst_ref=dst, send_sem=ss, recv_sem=rs, device_id=(dev_d, dev_t), device_id_type=MESH
        )

    def await_bytes(ref, sem):
        pltpu.make_async_copy(ref, ref, sem).wait()

    def rows16(i):
        return pl.ds(pl.multiple_of(i * 16, 16), 16)

    def peer64(j):
        return lax.rem(z + j % 4, 4) , lax.rem(t + j // 4, 16)

    barrier = pltpu.get_barrier_semaphore()

    def greet(j, carry):
        zz, tt = peer64(j)
        pl.semaphore_signal(barrier, inc=1, device_id=(zz * 4 + y, tt), device_id_type=MESH)
        return carry

    lax.fori_loop(1, 64, greet, 0)
    for zz in range(4):
        pl.semaphore_signal(barrier, inc=1, device_id=(zz * 4 + y + 1 - 2 * yi, t), device_id_type=MESH)
    pl.semaphore_signal(barrier, inc=1, device_id=(d_c, t), device_id_type=MESH)

    def hidden_step(i, carry):
        rows = rows16(i)
        for q in range(7):
            cols = slice(256 * q, 256 * q + 256)
            g = gate_ref[rows, cols].astype(F32)
            u = up_ref[rows, cols].astype(F32)
            hid[rows, cols] = (g * jax.nn.sigmoid(g) * u).astype(BF16)
        return carry

    lax.fori_loop(0, 8, hidden_step, 0)
    for q in range(7):
        turned = dot(hid[:, 256 * q : 256 * q + 256], h256_ref[...], 1, 0).astype(BF16)
        hs[0, q] = turned[:, :128]
        hs[1, q] = turned[:, 128:]

    pl.semaphore_wait(barrier, 68)

    def columns(zz, yy, c):
        low = yy - (yy // 2) * (2 * yy - 3)
        return pl.ds(pl.multiple_of(512 * (zz * 4 + low + c * (3 - 2 * low)), 512), 512)

    def send_d1(j, carry):
        zz = lax.rem(z + j // 2, 4)
        yy = y - yi + lax.rem(yi + j % 2, 2)
        for c in range(2):
            remote(
                dy_ref.at[rows16(part), columns(zz, yy, c)],
                dyb.at[yi, z, rows16(part), pl.ds(512 * c, 512)],
                s_d1s, s_d1r, zz * 4 + yy, t,
            ).start()
        return carry

    for c in range(2):
        pltpu.make_async_copy(
            dy_ref.at[rows16(part), columns(z, y, c)], dyb.at[yi, z, rows16(part), pl.ds(512 * c, 512)], s_d1r
        ).start()
    lax.fori_loop(1, 8, send_d1, 0)

    def send_h1(k, carry):
        p = lax.rem(t + k, 16)
        remote(hs.at[p % 2, :, rows16(p // 2), :], h1.at[pl.ds(7 * t, 7)], s_h1s, s_h1r, d, p).start()
        return carry

    pltpu.make_async_copy(hs.at[lh, :, rows16(tg), :], h1.at[pl.ds(7 * t, 7)], s_h1r).start()
    lax.fori_loop(1, 16, send_h1, 0)

    def quant_group(g, carry):
        step = step_ref[pl.ds(g, 1), :]
        inverse = 1.0 / step

        def chunk(i, inner):
            rows = rows16(g * 16 + i)
            ratios = dw_ref[rows, :].astype(F32) * inverse
            clipped = jnp.clip(ratios, -8.0, 7.0)
            r = clipped - jnp.round(clipped)
            u = r * r
            s = r * horner(sin_series, u)
            c = horner(cos_series, u)
            levels = clipped - s * c * (1.0 / math.pi)
            slope = 2.0 * s * s
            slopes[rows, :] = slope
            extra[rows, :] = levels - ratios * slope
            qb[di, g, rows16(i), :] = (step * levels).astype(BF16)
            return inner

        lax.fori_loop(0, 16, chunk, 0)
        remote(qb.at[di, g], qb.at[di, g], s_qs.at[g], s_qr.at[g], d_c, t).start()
        return carry

    lax.fori_loop(0, 7, quant_group, 0)

    await_bytes(dyb.at[0, :, 0:32, :], s_d1r)

    sibling = t + 1 - 2 * lh

    def d2_block(k):
        return dyb.at[:, :, rows16(lax.rem(part + 2 * k, 8)), :]

    def send_d2(k, carry):
        p = hi8 + lax.rem(part + 2 * k, 8)
        remote(d2_block(0), d2_block(0), s_d2s, s_d2r.at[k], d, p).start()
        return carry

    lax.fori_loop(1, 4, send_d2, 0)
    remote(d2_block(0), d2_block(0), s_d3s, s_d3r, d, sibling).start()

    await_bytes(h1, s_h1r)

    def spread_h(a, carry):
        x = [h1[a * 4 + b].astype(F32) for b in range(4)]
        p0, p1, m0, m1 = x[0] + x[1], x[2] + x[3], x[0] - x[1], x[2] - x[3]
        mixf[0, a] = p0 + p1
        mixf[1, a] = m0 + m1
        mixf[2, a] = p0 - p1
        mixf[3, a] = m0 - m1
        return carry

    lax.fori_loop(0, 28, spread_h, 0)
    mix_paley(paley, mixf, h2, SCALE)

    def h_place(zz, ti, chunk):
        q0, n = CHUNKS[chunk]
        return hb.at[yi, ti % 2, q0 : q0 + n, pl.ds(pl.multiple_of(zz * 128 + (ti // 2) * 16, 16), 16), :]

    def push_h(chunk):
        q0, n = CHUNKS[chunk]

        def send_h2(j, carry):
            zz, tt = peer64(j)
            remote(
                h2.at[pl.ds(7 * tt + q0, n)], h_place(z, t, chunk), s_h2s, s_h2r.at[chunk, z], zz * 4 + y, tt
            ).start()
            return carry

        pltpu.make_async_copy(h2.at[pl.ds(7 * t + q0, n)], h_place(z, t, chunk), s_h2r.at[chunk, z]).start()
        lax.fori_loop(1, 64, send_h2, 0)

    push_h(0)

    def forward_d3(k, carry):
        block = d2_block(4 - k)
        await_bytes(block, s_d2r.at[k])
        remote(block, block, s_d3s, s_d3r, d, sibling).start()
        return carry

    lax.fori_loop(1, 4, forward_d3, 0)
    push_h(1)

    await_bytes(dyb.at[:, :, 0:64, :], s_d3r)

    def product_g(which, g):
        total = dot(dyb[which, :, :, :512].reshape(512, 512), qb[0, g], 1, 1)
        return total + dot(dyb[which, :, :, 512:].reshape(512, 512), qb[1, g], 1, 1)

    def grad_group(g, carry):
        remote(qb.at[di, g], qb.at[do, g], s_qs.at[g], s_qr.at[g], d_c, t).wait_recv()
        theirs = product_g(yo, g).astype(BF16)
        gsend[g, 0] = theirs[:, :128]
        gsend[g, 1] = theirs[:, 128:]
        remote(gsend.at[g], gx.at[g], s_gxs.at[g], s_gxr.at[g], d_t, t).start()
        ours = product_g(yi, g).astype(BF16)
        gsum[0, g] = ours[:, :128]
        gsum[1, g] = ours[:, 128:]
        return carry

    lax.fori_loop(0, 4, grad_group, 0)

    def h_block(which, zz, chunk):
        q0, n = CHUNKS[chunk]
        return hb.at[which, :, q0 : q0 + n, pl.ds(pl.multiple_of(zz * 128, 128), 128), :]

    def h_pass(k, chunk, which):
        zz = lax.rem(z + k, 4)
        return remote(
            h_block(yi, zz, chunk), h_block(which, zz, chunk), s_hxs.at[chunk, k], s_hxr.at[chunk, k], d_t, t
        )

    def forward_h(chunk):
        def step(k, carry):
            zz = lax.rem(z + k, 4)
            await_bytes(h_block(yi, zz, chunk), s_h2r.at[chunk, zz])
            h_pass(k, chunk, yi).start()
            return carry

        lax.fori_loop(0, 4, step, 0)

    forward_h(0)
    lax.fori_loop(4, 7, grad_group, 0)

    def add_group(g, carry):
        remote(gsend.at[g], gx.at[g], s_gxs.at[g], s_gxr.at[g], d_t, t).wait_recv()

        def chunk(i, inner):
            rows = pl.ds(pl.multiple_of(i * 64, 64), 64)
            for k in range(2):
                gsum[k, g, rows, :] = (gsum[k, g, rows, :].astype(F32) + gx[g, k, rows, :].astype(F32)).astype(BF16)
            return inner

        return lax.fori_loop(0, 8, chunk, carry)

    lax.fori_loop(0, 7, add_group, 0)

    def g_piece(zz, ti):
        return gsum.at[ti % 2, :, pl.ds(pl.multiple_of(zz * 128 + (ti // 2) * 16, 16), 16), :]

    def g_place(zz, ti):
        return gr.at[pl.ds(zz * 112 + 7 * ti, 7)]

    def send_gr(j, carry):
        zz, tt = peer64(j)
        remote(g_piece(zz, tt), g_place(z, t), s_grs, s_grr, zz * 4 + y, tt).start()
        return carry

    pltpu.make_async_copy(g_piece(z, t), g_place(z, t), s_grr).start()
    lax.fori_loop(1, 64, send_gr, 0)

    forward_h(1)

    def product_d(q, half, c):
        cols = pl.ds(pl.multiple_of(c * 512, 512), 512)
        total = dot(hb[0, half, q], dyb[0, :, :, cols].reshape(512, 512), 0, 0)
        return total + dot(hb[1, half, q], dyb[1, :, :, cols].reshape(512, 512), 0, 0)

    def weight_group(q, carry):
        for half in range(2):
            dsend[q, 128 * half : 128 * half + 128, :] = product_d(q, half, do).astype(BF16)
        remote(dsend.at[q], dx.at[q], s_xs.at[q], s_xr.at[q], d_c, t).start()
        for half in range(2):
            wg_ref[pl.ds(pl.multiple_of(q * 256 + 128 * half, 128), 128), :] = product_d(q, half, di)
        return carry

    for chunk, (q0, n) in enumerate(CHUNKS):

        def receive_h(k, carry, chunk=chunk):
            h_pass(k, chunk, yo).wait_recv()
            return carry

        lax.fori_loop(0, 4, receive_h, 0)
        lax.fori_loop(q0, q0 + n, weight_group, 0)

    await_bytes(gr, s_grr)

    def spread_g(a, carry):
        x = []
        for b in range(4):
            total = gr[a * 4 + b].astype(F32)
            for zz in range(1, 4):
                total = total + gr[112 * zz + a * 4 + b].astype(F32)
            x.append(total)
        p0, p1, m0, m1 = x[0] + x[1], x[2] + x[3], x[0] - x[1], x[2] - x[3]
        mixf[0, a] = p0 + p1
        mixf[1, a] = m0 + m1
        mixf[2, a] = p0 - p1
        mixf[3, a] = m0 - m1
        return carry

    lax.fori_loop(0, 28, spread_g, 0)
    mix_paley(paley.T, mixf, gm, SCALE)

    def f_place(ti):
        return fr.at[ti % 2, :, rows16(ti // 2), :]

    def send_f(k, carry):
        p = lax.rem(t + k, 16)
        remote(gm.at[pl.ds(7 * p, 7)], f_place(t), s_fs, s_fr, d, p).start()
        return carry

    pltpu.make_async_copy(gm.at[pl.ds(7 * t, 7)], f_place(t), s_fr).start()
    lax.fori_loop(1, 16, send_f, 0)
    def weight_finish(q, carry):
        remote(dsend.at[q], dx.at[q], s_xs.at[q], s_xr.at[q], d_c, t).wait_recv()

        def chunk(i, acc):
            rows = rows16(q * 16 + i)
            total = wg_ref[rows, :] + dx[q, rows16(i), :].astype(F32)
            wg_ref[rows, :] = total * slopes[rows, :]
            return acc + total * extra[rows, :]

        acc = lax.fori_loop(0, 16, chunk, jnp.zeros((16, 512), F32))
        sg_ref[pl.ds(q, 1), :] = jnp.sum(acc, axis=0, keepdims=True) * (1.0 / math.sqrt(1792.0))
        return carry

    lax.fori_loop(0, 7, weight_finish, 0)
    await_bytes(fr, s_fr)

    await_bytes(h1.at[0:105], s_h1s)
    await_bytes(gr.at[0:441], s_h2s)
    await_bytes(gr.at[0:441], s_grs)
    await_bytes(gm.at[0:105], s_fs)
    await_bytes(dyb.at[0, 0, 0:112, :], s_d1s)
    await_bytes(dyb.at[:, :, 0:48, :], s_d2s)
    await_bytes(dyb.at[:, :, 0:64, :], s_d3s)

    def drain7(g, carry):
        remote(qb.at[di, g], qb.at[di, g], s_qs.at[g], s_qr.at[g], d_c, t).wait_send()
        remote(gsend.at[g], gx.at[g], s_gxs.at[g], s_gxr.at[g], d_t, t).wait_send()
        remote(dsend.at[g], dx.at[g], s_xs.at[g], s_xr.at[g], d_c, t).wait_send()
        return carry

    lax.fori_loop(0, 7, drain7, 0)

    def drain4(k, carry):
        for chunk in range(2):
            h_pass(k, chunk, yi).wait_send()
        return carry

    lax.fori_loop(0, 4, drain4, 0)


def finish_kernel(
    gate_in, up_in, h256_in, fr_in, wg_in, sg_in, dgate_ref, dup_ref, wg_out, sg_out, gate, up, h256, fr, wg, sg, gh, sem
):
    bring = [
        pltpu.make_async_copy(src, dst, sem.at[i])
        for i, (src, dst) in enumerate(
            ((wg_in, wg), (fr_in, fr), (h256_in, h256), (gate_in, gate), (up_in, up), (sg_in, sg))
        )
    ]
    for copy in bring:
        copy.start()
    for copy in bring[1:]:
        copy.wait()
    sg_out[...] = sg[...]
    bring[0].wait()
    move = pltpu.make_async_copy(wg, wg_out, sem.at[0])
    move.start()
    for q in range(7):
        gh[...] = dot(fr[0, q], h256[:128, :], 1, 0) + dot(fr[1, q], h256[128:, :], 1, 0)
        cols = slice(256 * q, 256 * q + 256)

        def step(i, carry, cols=cols):
            rows = pl.ds(pl.multiple_of(i * 16, 16), 16)
            g = gate[rows, cols].astype(F32)
            u = up[rows, cols].astype(F32)
            sig = jax.nn.sigmoid(g)
            grad = gh[rows, :] * sig
            dup_ref[rows, cols] = (grad * g).astype(BF16)
            dgate_ref[rows, cols] = (grad * u * (1.0 + g * (1.0 - sig))).astype(BF16)
            return carry

        lax.fori_loop(0, 8, step, 0)
    move.wait()


def shards(d_out, gate_pre, up_pre, down_weight, step_size):
    h256 = jnp.asarray(sylvester(256), BF16)
    vmem = pl.BlockSpec(memory_space=pltpu.VMEM)
    dma = pltpu.SemaphoreType.DMA
    fr, weight, step = pl.pallas_call(
        kernel,
        out_shape=(
            jax.ShapeDtypeStruct((2, 7, 128, 128), BF16),
            jax.ShapeDtypeStruct((1792, 512), F32),
            jax.ShapeDtypeStruct((7, 512), F32),
        ),
        in_specs=[pl.BlockSpec(memory_space=pl.ANY)] + [vmem] * 5,
        out_specs=(vmem,) * 3,
        scratch_shapes=[
            pltpu.VMEM((128, 1792), BF16),
            pltpu.VMEM((2, 7, 128, 128), BF16),
            pltpu.VMEM((112, 16, 128), BF16),
            pltpu.VMEM((8, 28, 16, 128), F32),
            pltpu.VMEM((112, 16, 128), BF16),
            pltpu.VMEM((2, 2, 7, 512, 128), BF16),
            pltpu.VMEM((2, 4, 128, 1024), BF16),
            pltpu.VMEM((2, 7, 256, 512), BF16),
            pltpu.VMEM((1792, 512), F32),
            pltpu.VMEM((1792, 512), F32),
            pltpu.VMEM((7, 2, 512, 128), BF16),
            pltpu.VMEM((7, 2, 512, 128), BF16),
            pltpu.VMEM((2, 7, 512, 128), BF16),
            pltpu.VMEM((448, 16, 128), BF16),
            pltpu.VMEM((112, 16, 128), BF16),
            pltpu.VMEM((7, 256, 512), BF16),
            pltpu.VMEM((7, 256, 512), BF16),
            dma, dma,
            dma, dma((2, 4)),
            dma((2, 4)), dma((2, 4)),
            dma, dma,
            dma, dma((4,)),
            dma, dma,
            dma((7,)), dma((7,)),
            dma((7,)), dma((7,)),
            dma, dma,
            dma, dma,
            dma((7,)), dma((7,)),
        ],
        compiler_params=pltpu.CompilerParams(
            collective_id=0, has_side_effects=True, vmem_limit_bytes=58 * 1024 * 1024
        ),
        cost_estimate=pl.CostEstimate(flops=8_000_000_000, bytes_accessed=12_000_000, transcendentals=1_000_000),
    )(d_out, gate_pre, up_pre, down_weight, step_size, h256)
    anywhere = pl.BlockSpec(memory_space=pl.ANY)
    return pl.pallas_call(
        finish_kernel,
        out_shape=(
            jax.ShapeDtypeStruct((128, 1792), BF16),
            jax.ShapeDtypeStruct((128, 1792), BF16),
            jax.ShapeDtypeStruct((1792, 512), F32),
            jax.ShapeDtypeStruct((7, 512), F32),
        ),
        in_specs=[anywhere] * 6,
        out_specs=(vmem, vmem, anywhere, vmem),
        scratch_shapes=[
            pltpu.VMEM((128, 1792), BF16),
            pltpu.VMEM((128, 1792), BF16),
            pltpu.VMEM((256, 256), BF16),
            pltpu.VMEM((2, 7, 128, 128), BF16),
            pltpu.VMEM((1792, 512), F32),
            pltpu.VMEM((7, 512), F32),
            pltpu.VMEM((128, 256), F32),
            dma((6,)),
        ],
        compiler_params=pltpu.CompilerParams(vmem_limit_bytes=60 * 1024 * 1024),
        cost_estimate=pl.CostEstimate(flops=200_000_000, bytes_accessed=10_000_000, transcendentals=300_000),
    )(gate_pre, up_pre, h256, fr, weight, step)


def solution(mesh):
    return jax.shard_map(
        shards,
        mesh=mesh,
        in_specs=(
            P("dp", None),
            P("dp", "tensor"),
            P("dp", "tensor"),
            P("tensor", "dp"),
            P("tensor", "dp"),
        ),
        out_specs=(P("dp", "tensor"), P("dp", "tensor"), P("tensor", "dp"), P("tensor", "dp")),
        check_vma=False,
    )
```

```python
import math

import jax
import jax.numpy as jnp
import numpy as np
from jax import lax
from jax.experimental import pallas as pl
from jax.experimental.pallas import tpu as pltpu
from jax.sharding import PartitionSpec as P

FF = 28672
F32, BF16 = jnp.float32, jnp.bfloat16
MESH = pl.DeviceIdType.MESH
SCALE = 1.0 / math.sqrt(FF)
CHUNKS = ((0, 4), (4, 3))


def paley_matrix():
    digits_of = [(number % 3, number // 3 % 3, number // 9) for number in range(27)]
    lookup = {digits: number for number, digits in enumerate(digits_of)}

    def field_product(left_poly, right_poly):
        coeffs = [0, 0, 0, 0, 0]
        for left_pos in range(3):
            for right_pos in range(3):
                coeffs[left_pos + right_pos] += left_poly[left_pos] * right_poly[right_pos]
        for degree in (4, 3):
            excess = coeffs[degree]
            coeffs[degree] = 0
            coeffs[degree - 2] += excess
            coeffs[degree - 3] += 2 * excess
        return tuple((coefficient % 3 for coefficient in coeffs[:3]))

    squares_set = set((lookup[field_product(digits, digits)] for digits in digits_of[1:]))
    matrix_out = np.eye(28, dtype=np.float32)
    matrix_out[0, 1:] += 1.0
    matrix_out[1:, 0] -= 1.0
    for row_num in range(27):
        for col_num in range(27):
            if row_num != col_num:
                diff_poly = tuple(
                    (
                        (digits_of[row_num][position] - digits_of[col_num][position]) % 3
                        for position in range(3)
                    )
                )
                matrix_out[row_num + 1, col_num + 1] += (
                    1.0 if lookup[diff_poly] in squares_set else -1.0
                )
    return matrix_out


def sylvester(order_size):
    indices = np.arange(order_size)
    anded = indices[:, None] & indices[None, :]
    parity = np.zeros((order_size, order_size), np.int64)
    for bit_num in range(int(order_size).bit_length()):
        parity = parity + (anded >> bit_num & 1)
    return (1 - 2 * (parity % 2)).astype(np.float32)


def half_turn_series():
    points = 0.125 - 0.125 * np.cos((np.arange(64) + 0.5) * np.pi / 64)
    root = np.sqrt(points)
    a = np.polyfit(points, np.sin(np.pi * root) / root, 5)
    b = np.polyfit(points, np.cos(np.pi * root), 6)
    return [float(v) for v in a], [float(v) for v in b]


def horner(coefficients, u):
    total = coefficients[0] * u + coefficients[1]
    for c in coefficients[2:]:
        total = total * u + c
    return total


def dot(a, b, ca, cb):
    return lax.dot_general(a, b, (((ca,), (cb,)), ((), ())), preferred_element_type=F32)


def mix_paley(paley, src, dst, scale):
    def step(b, carry):
        for half in range(2):
            rows = slice(8 * half, 8 * half + 8)
            x = [src[b, a, rows, :] for a in range(28)]
            whole = x
            while len(whole) > 1:
                whole = [whole[i] + whole[i + 1] if i + 1 < len(whole) else whole[i] for i in range(0, len(whole), 2)]
            for c in range(28):
                negative = [x[a] for a in range(28) if paley[a, c] < 0]
                if negative:
                    less = negative[0]
                    for n in negative[1:]:
                        less = less + n
                    src[4 + b, c, rows, :] = (whole[0] - 2.0 * less) * scale
                else:
                    src[4 + b, c, rows, :] = whole[0] * scale
        for c in range(28):
            dst[c * 4 + b] = src[4 + b, c].astype(BF16)
        return carry

    lax.fori_loop(0, 4, step, 0)


def kernel(
    dy_ref, gate_ref, up_ref, dw_ref, step_ref, h256_ref,
    fr, wg_ref, sg_ref,
    hid, hs, h1, mixf, h2, hb, dyb, qb, slopes, extra, gsend, gx, gsum, gr, gm, dsend, dx,
    s_h1s, s_h1r, s_h2s, s_h2r, s_hxs, s_hxr, s_d1s, s_d1r, s_d2s, s_d2r, s_d3s, s_d3r, s_qs, s_qr,
    s_gxs, s_gxr, s_grs, s_grr, s_fs, s_fr, s_xs, s_xr,
):
    paley = paley_matrix()
    sin_series, cos_series = half_turn_series()
    d, t = lax.axis_index("dp"), lax.axis_index("tensor")
    z, y = d // 4, d % 4
    yi = y % 2
    yo = 1 - yi
    d_t = z * 4 + y + 1 - 2 * yi
    d_c = z * 4 + 3 - y
    di = y // 2
    do = 1 - di
    tg, lh = t // 2, t % 2
    part = t % 8
    hi8 = t - part

    def remote(src, dst, ss, rs, dev_d, dev_t):
        return pltpu.make_async_remote_copy(
            src_ref=src, dst_ref=dst, send_sem=ss, recv_sem=rs, device_id=(dev_d, dev_t), device_id_type=MESH
        )

    def await_bytes(ref, sem):
        pltpu.make_async_copy(ref, ref, sem).wait()

    def rows16(i):
        return pl.ds(pl.multiple_of(i * 16, 16), 16)

    def peer64(j):
        return lax.rem(z + j % 4, 4) , lax.rem(t + j // 4, 16)

    barrier = pltpu.get_barrier_semaphore()

    def greet(j, carry):
        zz, tt = peer64(j)
        pl.semaphore_signal(barrier, inc=1, device_id=(zz * 4 + y, tt), device_id_type=MESH)
        return carry

    lax.fori_loop(1, 64, greet, 0)
    for zz in range(4):
        pl.semaphore_signal(barrier, inc=1, device_id=(zz * 4 + y + 1 - 2 * yi, t), device_id_type=MESH)
    pl.semaphore_signal(barrier, inc=1, device_id=(d_c, t), device_id_type=MESH)

    def hidden_step(i, carry):
        rows = rows16(i)
        for q in range(7):
            cols = slice(256 * q, 256 * q + 256)
            g = gate_ref[rows, cols].astype(F32)
            u = up_ref[rows, cols].astype(F32)
            hid[rows, cols] = (g * jax.nn.sigmoid(g) * u).astype(BF16)
        return carry

    lax.fori_loop(0, 8, hidden_step, 0)
    for q in range(7):
        turned = dot(hid[:, 256 * q : 256 * q + 256], h256_ref[...], 1, 0).astype(BF16)
        hs[0, q] = turned[:, :128]
        hs[1, q] = turned[:, 128:]

    pl.semaphore_wait(barrier, 68)

    def columns(zz, yy, c):
        low = yy - (yy // 2) * (2 * yy - 3)
        return pl.ds(pl.multiple_of(512 * (zz * 4 + low + c * (3 - 2 * low)), 512), 512)

    def send_d1(j, carry):
        zz = lax.rem(z + j // 2, 4)
        yy = y - yi + lax.rem(yi + j % 2, 2)
        for c in range(2):
            remote(
                dy_ref.at[rows16(part), columns(zz, yy, c)],
                dyb.at[yi, z, rows16(part), pl.ds(512 * c, 512)],
                s_d1s, s_d1r, zz * 4 + yy, t,
            ).start()
        return carry

    for c in range(2):
        pltpu.make_async_copy(
            dy_ref.at[rows16(part), columns(z, y, c)], dyb.at[yi, z, rows16(part), pl.ds(512 * c, 512)], s_d1r
        ).start()
    lax.fori_loop(1, 8, send_d1, 0)

    def send_h1(k, carry):
        p = lax.rem(t + k, 16)
        remote(hs.at[p % 2, :, rows16(p // 2), :], h1.at[pl.ds(7 * t, 7)], s_h1s, s_h1r, d, p).start()
        return carry

    pltpu.make_async_copy(hs.at[lh, :, rows16(tg), :], h1.at[pl.ds(7 * t, 7)], s_h1r).start()
    lax.fori_loop(1, 16, send_h1, 0)

    def quant_group(g, carry):
        step = step_ref[pl.ds(g, 1), :]
        inverse = 1.0 / step

        def chunk(i, inner):
            rows = rows16(g * 16 + i)
            ratios = dw_ref[rows, :].astype(F32) * inverse
            clipped = jnp.clip(ratios, -8.0, 7.0)
            r = clipped - jnp.round(clipped)
            u = r * r
            s = r * horner(sin_series, u)
            c = horner(cos_series, u)
            levels = clipped - s * c * (1.0 / math.pi)
            slope = 2.0 * s * s
            slopes[rows, :] = slope
            extra[rows, :] = levels - ratios * slope
            qb[di, g, rows16(i), :] = (step * levels).astype(BF16)
            return inner

        lax.fori_loop(0, 16, chunk, 0)
        remote(qb.at[di, g], qb.at[di, g], s_qs.at[g], s_qr.at[g], d_c, t).start()
        return carry

    lax.fori_loop(0, 7, quant_group, 0)

    await_bytes(dyb.at[0, :, 0:32, :], s_d1r)

    sibling = t + 1 - 2 * lh

    def d2_block(k):
        return dyb.at[:, :, rows16(lax.rem(part + 2 * k, 8)), :]

    def send_d2(k, carry):
        p = hi8 + lax.rem(part + 2 * k, 8)
        remote(d2_block(0), d2_block(0), s_d2s, s_d2r.at[k], d, p).start()
        return carry

    lax.fori_loop(1, 4, send_d2, 0)
    remote(d2_block(0), d2_block(0), s_d3s, s_d3r, d, sibling).start()

    await_bytes(h1, s_h1r)

    def spread_h(a, carry):
        x = [h1[a * 4 + b].astype(F32) for b in range(4)]
        p0, p1, m0, m1 = x[0] + x[1], x[2] + x[3], x[0] - x[1], x[2] - x[3]
        mixf[0, a] = p0 + p1
        mixf[1, a] = m0 + m1
        mixf[2, a] = p0 - p1
        mixf[3, a] = m0 - m1
        return carry

    lax.fori_loop(0, 28, spread_h, 0)
    mix_paley(paley, mixf, h2, SCALE)

    def h_place(zz, ti):
        return hb.at[yi, ti % 2, :, pl.ds(pl.multiple_of(zz * 128 + (ti // 2) * 16, 16), 16), :]

    def send_h2(j, carry):
        zz, tt = peer64(j)
        remote(h2.at[pl.ds(7 * tt, 7)], h_place(z, t), s_h2s, s_h2r, zz * 4 + y, tt).start()
        return carry

    pltpu.make_async_copy(h2.at[pl.ds(7 * t, 7)], h_place(z, t), s_h2r).start()
    lax.fori_loop(1, 64, send_h2, 0)

    def forward_d3(k, carry):
        block = d2_block(4 - k)
        await_bytes(block, s_d2r.at[k])
        remote(block, block, s_d3s, s_d3r, d, sibling).start()
        return carry

    lax.fori_loop(1, 4, forward_d3, 0)

    await_bytes(dyb.at[:, :, 0:64, :], s_d3r)

    def product_g(which, g):
        total = dot(dyb[which, :, :, :512].reshape(512, 512), qb[0, g], 1, 1)
        return total + dot(dyb[which, :, :, 512:].reshape(512, 512), qb[1, g], 1, 1)

    def grad_group(g, carry):
        remote(qb.at[di, g], qb.at[do, g], s_qs.at[g], s_qr.at[g], d_c, t).wait_recv()
        theirs = product_g(yo, g).astype(BF16)
        gsend[g, 0] = theirs[:, :128]
        gsend[g, 1] = theirs[:, 128:]
        remote(gsend.at[g], gx.at[g], s_gxs.at[g], s_gxr.at[g], d_t, t).start()
        ours = product_g(yi, g).astype(BF16)
        gsum[0, g] = ours[:, :128]
        gsum[1, g] = ours[:, 128:]
        return carry

    lax.fori_loop(0, 7, grad_group, 0)

    def add_group(g, carry):
        remote(gsend.at[g], gx.at[g], s_gxs.at[g], s_gxr.at[g], d_t, t).wait_recv()

        def chunk(i, inner):
            rows = pl.ds(pl.multiple_of(i * 64, 64), 64)
            for k in range(2):
                gsum[k, g, rows, :] = (gsum[k, g, rows, :].astype(F32) + gx[g, k, rows, :].astype(F32)).astype(BF16)
            return inner

        return lax.fori_loop(0, 8, chunk, carry)

    def push_g(chunk):
        q0, n = CHUNKS[chunk]

        def piece(zz, ti):
            return gsum.at[ti % 2, q0 : q0 + n, pl.ds(pl.multiple_of(zz * 128 + (ti // 2) * 16, 16), 16), :]

        place = gr.at[pl.ds(z * 112 + 7 * t + q0, n)]

        def send_gr(j, carry):
            zz, tt = peer64(j)
            remote(piece(zz, tt), place, s_grs, s_grr, zz * 4 + y, tt).start()
            return carry

        lax.fori_loop(q0, q0 + n, add_group, 0)
        pltpu.make_async_copy(piece(z, t), place, s_grr).start()
        lax.fori_loop(1, 64, send_gr, 0)

    push_g(0)

    def h_pass(q, which):
        return remote(hb.at[yi, :, q], hb.at[which, :, q], s_hxs.at[q], s_hxr.at[q], d_t, t)

    def forward_h(q, carry):
        h_pass(q, yi).start()
        return carry

    await_bytes(hb.at[yi], s_h2r)
    lax.fori_loop(0, 7, forward_h, 0)
    push_g(1)

    def product_d(q, half, c):
        cols = pl.ds(pl.multiple_of(c * 512, 512), 512)
        total = dot(hb[0, half, q], dyb[0, :, :, cols].reshape(512, 512), 0, 0)
        return total + dot(hb[1, half, q], dyb[1, :, :, cols].reshape(512, 512), 0, 0)

    def weight_group(q, carry):
        h_pass(q, yo).wait_recv()
        for half in range(2):
            dsend[q, 128 * half : 128 * half + 128, :] = product_d(q, half, do).astype(BF16)
        remote(dsend.at[q], dx.at[q], s_xs.at[q], s_xr.at[q], d_c, t).start()
        for half in range(2):
            wg_ref[pl.ds(pl.multiple_of(q * 256 + 128 * half, 128), 128), :] = product_d(q, half, di)
        return carry

    lax.fori_loop(0, 7, weight_group, 0)

    await_bytes(gr, s_grr)

    def spread_g(a, carry):
        x = []
        for b in range(4):
            total = gr[a * 4 + b].astype(F32)
            for zz in range(1, 4):
                total = total + gr[112 * zz + a * 4 + b].astype(F32)
            x.append(total)
        p0, p1, m0, m1 = x[0] + x[1], x[2] + x[3], x[0] - x[1], x[2] - x[3]
        mixf[0, a] = p0 + p1
        mixf[1, a] = m0 + m1
        mixf[2, a] = p0 - p1
        mixf[3, a] = m0 - m1
        return carry

    lax.fori_loop(0, 28, spread_g, 0)
    mix_paley(paley.T, mixf, gm, SCALE)

    def f_place(ti):
        return fr.at[ti % 2, :, rows16(ti // 2), :]

    def send_f(k, carry):
        p = lax.rem(t + k, 16)
        remote(gm.at[pl.ds(7 * p, 7)], f_place(t), s_fs, s_fr, d, p).start()
        return carry

    pltpu.make_async_copy(gm.at[pl.ds(7 * t, 7)], f_place(t), s_fr).start()
    lax.fori_loop(1, 16, send_f, 0)
    def weight_finish(q, carry):
        remote(dsend.at[q], dx.at[q], s_xs.at[q], s_xr.at[q], d_c, t).wait_recv()

        def chunk(i, acc):
            rows = rows16(q * 16 + i)
            total = wg_ref[rows, :] + dx[q, rows16(i), :].astype(F32)
            wg_ref[rows, :] = total * slopes[rows, :]
            return acc + total * extra[rows, :]

        acc = lax.fori_loop(0, 16, chunk, jnp.zeros((16, 512), F32))
        sg_ref[pl.ds(q, 1), :] = jnp.sum(acc, axis=0, keepdims=True) * (1.0 / math.sqrt(1792.0))
        return carry

    lax.fori_loop(0, 7, weight_finish, 0)
    await_bytes(fr, s_fr)

    await_bytes(h1.at[0:105], s_h1s)
    await_bytes(gr.at[0:441], s_h2s)
    await_bytes(gr.at[0:441], s_grs)
    await_bytes(gm.at[0:105], s_fs)
    await_bytes(dyb.at[0, 0, 0:112, :], s_d1s)
    await_bytes(dyb.at[:, :, 0:48, :], s_d2s)
    await_bytes(dyb.at[:, :, 0:64, :], s_d3s)

    def drain7(g, carry):
        remote(qb.at[di, g], qb.at[di, g], s_qs.at[g], s_qr.at[g], d_c, t).wait_send()
        remote(gsend.at[g], gx.at[g], s_gxs.at[g], s_gxr.at[g], d_t, t).wait_send()
        remote(dsend.at[g], dx.at[g], s_xs.at[g], s_xr.at[g], d_c, t).wait_send()
        h_pass(g, yi).wait_send()
        return carry

    lax.fori_loop(0, 7, drain7, 0)


def finish_kernel(
    gate_in, up_in, h256_in, fr_in, wg_in, sg_in, dgate_ref, dup_ref, wg_out, sg_out, gate, up, h256, fr, wg, sg, gh, sem
):
    bring = [
        pltpu.make_async_copy(src, dst, sem.at[i])
        for i, (src, dst) in enumerate(
            ((wg_in, wg), (fr_in, fr), (h256_in, h256), (gate_in, gate), (up_in, up), (sg_in, sg))
        )
    ]
    for copy in bring:
        copy.start()
    for copy in bring[1:]:
        copy.wait()
    sg_out[...] = sg[...]
    bring[0].wait()
    move = pltpu.make_async_copy(wg, wg_out, sem.at[0])
    move.start()
    for q in range(7):
        gh[...] = dot(fr[0, q], h256[:128, :], 1, 0) + dot(fr[1, q], h256[128:, :], 1, 0)
        cols = slice(256 * q, 256 * q + 256)

        def step(i, carry, cols=cols):
            rows = pl.ds(pl.multiple_of(i * 16, 16), 16)
            g = gate[rows, cols].astype(F32)
            u = up[rows, cols].astype(F32)
            sig = jax.nn.sigmoid(g)
            grad = gh[rows, :] * sig
            dup_ref[rows, cols] = (grad * g).astype(BF16)
            dgate_ref[rows, cols] = (grad * u * (1.0 + g * (1.0 - sig))).astype(BF16)
            return carry

        lax.fori_loop(0, 8, step, 0)
    move.wait()


def shards(d_out, gate_pre, up_pre, down_weight, step_size):
    h256 = jnp.asarray(sylvester(256), BF16)
    vmem = pl.BlockSpec(memory_space=pltpu.VMEM)
    dma = pltpu.SemaphoreType.DMA
    fr, weight, step = pl.pallas_call(
        kernel,
        out_shape=(
            jax.ShapeDtypeStruct((2, 7, 128, 128), BF16),
            jax.ShapeDtypeStruct((1792, 512), F32),
            jax.ShapeDtypeStruct((7, 512), F32),
        ),
        in_specs=[pl.BlockSpec(memory_space=pl.ANY)] + [vmem] * 5,
        out_specs=(vmem,) * 3,
        scratch_shapes=[
            pltpu.VMEM((128, 1792), BF16),
            pltpu.VMEM((2, 7, 128, 128), BF16),
            pltpu.VMEM((112, 16, 128), BF16),
            pltpu.VMEM((8, 28, 16, 128), F32),
            pltpu.VMEM((112, 16, 128), BF16),
            pltpu.VMEM((2, 2, 7, 512, 128), BF16),
            pltpu.VMEM((2, 4, 128, 1024), BF16),
            pltpu.VMEM((2, 7, 256, 512), BF16),
            pltpu.VMEM((1792, 512), F32),
            pltpu.VMEM((1792, 512), F32),
            pltpu.VMEM((7, 2, 512, 128), BF16),
            pltpu.VMEM((7, 2, 512, 128), BF16),
            pltpu.VMEM((2, 7, 512, 128), BF16),
            pltpu.VMEM((448, 16, 128), BF16),
            pltpu.VMEM((112, 16, 128), BF16),
            pltpu.VMEM((7, 256, 512), BF16),
            pltpu.VMEM((7, 256, 512), BF16),
            dma, dma,
            dma, dma,
            dma((7,)), dma((7,)),
            dma, dma,
            dma, dma((4,)),
            dma, dma,
            dma((7,)), dma((7,)),
            dma((7,)), dma((7,)),
            dma, dma,
            dma, dma,
            dma((7,)), dma((7,)),
        ],
        compiler_params=pltpu.CompilerParams(
            collective_id=0, has_side_effects=True, vmem_limit_bytes=58 * 1024 * 1024
        ),
        cost_estimate=pl.CostEstimate(flops=8_000_000_000, bytes_accessed=12_000_000, transcendentals=1_000_000),
    )(d_out, gate_pre, up_pre, down_weight, step_size, h256)
    anywhere = pl.BlockSpec(memory_space=pl.ANY)
    return pl.pallas_call(
        finish_kernel,
        out_shape=(
            jax.ShapeDtypeStruct((128, 1792), BF16),
            jax.ShapeDtypeStruct((128, 1792), BF16),
            jax.ShapeDtypeStruct((1792, 512), F32),
            jax.ShapeDtypeStruct((7, 512), F32),
        ),
        in_specs=[anywhere] * 6,
        out_specs=(vmem, vmem, anywhere, vmem),
        scratch_shapes=[
            pltpu.VMEM((128, 1792), BF16),
            pltpu.VMEM((128, 1792), BF16),
            pltpu.VMEM((256, 256), BF16),
            pltpu.VMEM((2, 7, 128, 128), BF16),
            pltpu.VMEM((1792, 512), F32),
            pltpu.VMEM((7, 512), F32),
            pltpu.VMEM((128, 256), F32),
            dma((6,)),
        ],
        compiler_params=pltpu.CompilerParams(vmem_limit_bytes=60 * 1024 * 1024),
        cost_estimate=pl.CostEstimate(flops=200_000_000, bytes_accessed=10_000_000, transcendentals=300_000),
    )(gate_pre, up_pre, h256, fr, weight, step)


def solution(mesh):
    return jax.shard_map(
        shards,
        mesh=mesh,
        in_specs=(
            P("dp", None),
            P("dp", "tensor"),
            P("dp", "tensor"),
            P("tensor", "dp"),
            P("tensor", "dp"),
        ),
        out_specs=(P("dp", "tensor"), P("dp", "tensor"), P("tensor", "dp"), P("tensor", "dp")),
        check_vma=False,
    )
```

```python
import math

import jax
import jax.numpy as jnp
import numpy as np
from jax import lax
from jax.experimental import pallas as pl
from jax.experimental.pallas import tpu as pltpu
from jax.sharding import PartitionSpec as P

FF = 28672
F32, BF16 = jnp.float32, jnp.bfloat16
MESH = pl.DeviceIdType.MESH
SCALE = 1.0 / math.sqrt(FF)
CHUNKS = ((0, 4), (4, 3))


def paley_matrix():
    digits_of = [(number % 3, number // 3 % 3, number // 9) for number in range(27)]
    lookup = {digits: number for number, digits in enumerate(digits_of)}

    def field_product(left_poly, right_poly):
        coeffs = [0, 0, 0, 0, 0]
        for left_pos in range(3):
            for right_pos in range(3):
                coeffs[left_pos + right_pos] += left_poly[left_pos] * right_poly[right_pos]
        for degree in (4, 3):
            excess = coeffs[degree]
            coeffs[degree] = 0
            coeffs[degree - 2] += excess
            coeffs[degree - 3] += 2 * excess
        return tuple((coefficient % 3 for coefficient in coeffs[:3]))

    squares_set = set((lookup[field_product(digits, digits)] for digits in digits_of[1:]))
    matrix_out = np.eye(28, dtype=np.float32)
    matrix_out[0, 1:] += 1.0
    matrix_out[1:, 0] -= 1.0
    for row_num in range(27):
        for col_num in range(27):
            if row_num != col_num:
                diff_poly = tuple(
                    (
                        (digits_of[row_num][position] - digits_of[col_num][position]) % 3
                        for position in range(3)
                    )
                )
                matrix_out[row_num + 1, col_num + 1] += (
                    1.0 if lookup[diff_poly] in squares_set else -1.0
                )
    return matrix_out


def sylvester(order_size):
    indices = np.arange(order_size)
    anded = indices[:, None] & indices[None, :]
    parity = np.zeros((order_size, order_size), np.int64)
    for bit_num in range(int(order_size).bit_length()):
        parity = parity + (anded >> bit_num & 1)
    return (1 - 2 * (parity % 2)).astype(np.float32)


def half_turn_series():
    points = 0.125 - 0.125 * np.cos((np.arange(64) + 0.5) * np.pi / 64)
    root = np.sqrt(points)
    a = np.polyfit(points, np.sin(np.pi * root) / root, 5)
    b = np.polyfit(points, np.cos(np.pi * root), 6)
    return [float(v) for v in a], [float(v) for v in b]


def horner(coefficients, u):
    total = coefficients[0] * u + coefficients[1]
    for c in coefficients[2:]:
        total = total * u + c
    return total


def dot(a, b, ca, cb):
    return lax.dot_general(a, b, (((ca,), (cb,)), ((), ())), preferred_element_type=F32)


def mix_paley(paley, src, dst, scale):
    def step(b, carry):
        for half in range(2):
            rows = slice(8 * half, 8 * half + 8)
            x = [src[b, a, rows, :] for a in range(28)]
            whole = x
            while len(whole) > 1:
                whole = [whole[i] + whole[i + 1] if i + 1 < len(whole) else whole[i] for i in range(0, len(whole), 2)]
            for c in range(28):
                negative = [x[a] for a in range(28) if paley[a, c] < 0]
                if negative:
                    less = negative[0]
                    for n in negative[1:]:
                        less = less + n
                    src[4 + b, c, rows, :] = (whole[0] - 2.0 * less) * scale
                else:
                    src[4 + b, c, rows, :] = whole[0] * scale
        for c in range(28):
            dst[c * 4 + b] = src[4 + b, c].astype(BF16)
        return carry

    lax.fori_loop(0, 4, step, 0)


def kernel(
    dy_ref, gate_ref, up_ref, dw_ref, step_ref, h256_ref,
    fr, wg_ref, sg_ref,
    hid, hs, h1, mixf, h2, hb, dyb, qb, slopes, extra, gsend, gx, gsum, gr, gm, dsend, dx,
    s_h1s, s_h1r, s_h2s, s_h2r, s_hxs, s_hxr, s_d1s, s_d1r, s_d2s, s_d2r, s_d3s, s_d3r, s_qs, s_qr,
    s_gxs, s_gxr, s_grs, s_grr, s_fs, s_fr, s_xs, s_xr,
):
    paley = paley_matrix()
    sin_series, cos_series = half_turn_series()
    d, t = lax.axis_index("dp"), lax.axis_index("tensor")
    z, y = d // 4, d % 4
    yi = y % 2
    yo = 1 - yi
    d_t = z * 4 + y + 1 - 2 * yi
    d_c = z * 4 + 3 - y
    di = y // 2
    do = 1 - di
    tg, lh = t // 2, t % 2
    part = t % 8
    hi8 = t - part

    def remote(src, dst, ss, rs, dev_d, dev_t):
        return pltpu.make_async_remote_copy(
            src_ref=src, dst_ref=dst, send_sem=ss, recv_sem=rs, device_id=(dev_d, dev_t), device_id_type=MESH
        )

    def await_bytes(ref, sem):
        pltpu.make_async_copy(ref, ref, sem).wait()

    def rows16(i):
        return pl.ds(pl.multiple_of(i * 16, 16), 16)

    def peer64(j):
        return lax.rem(z + j % 4, 4) , lax.rem(t + j // 4, 16)

    barrier = pltpu.get_barrier_semaphore()

    def greet(j, carry):
        zz, tt = peer64(j)
        pl.semaphore_signal(barrier, inc=1, device_id=(zz * 4 + y, tt), device_id_type=MESH)
        return carry

    lax.fori_loop(1, 64, greet, 0)
    for zz in range(4):
        pl.semaphore_signal(barrier, inc=1, device_id=(zz * 4 + y + 1 - 2 * yi, t), device_id_type=MESH)
    pl.semaphore_signal(barrier, inc=1, device_id=(d_c, t), device_id_type=MESH)

    def hidden_step(i, carry):
        rows = rows16(i)
        for q in range(7):
            cols = slice(256 * q, 256 * q + 256)
            g = gate_ref[rows, cols].astype(F32)
            u = up_ref[rows, cols].astype(F32)
            hid[rows, cols] = (g * jax.nn.sigmoid(g) * u).astype(BF16)
        return carry

    lax.fori_loop(0, 8, hidden_step, 0)
    for q in range(7):
        turned = dot(hid[:, 256 * q : 256 * q + 256], h256_ref[...], 1, 0).astype(BF16)
        hs[0, q] = turned[:, :128]
        hs[1, q] = turned[:, 128:]

    pl.semaphore_wait(barrier, 68)

    def columns(zz, yy, c):
        low = yy - (yy // 2) * (2 * yy - 3)
        return pl.ds(pl.multiple_of(512 * (zz * 4 + low + c * (3 - 2 * low)), 512), 512)

    def send_d1(other):
        yy = y - yi + (yo if other else yi)

        def step(j, carry):
            zz = lax.rem(z + j, 4)
            for c in range(2):
                remote(
                    dy_ref.at[rows16(part), columns(zz, yy, c)],
                    dyb.at[yi, z, rows16(part), pl.ds(512 * c, 512)],
                    s_d1s, s_d1r.at[other], zz * 4 + yy, t,
                ).start()
            return carry

        lax.fori_loop(1 - other, 4, step, 0)

    send_d1(1)
    for c in range(2):
        pltpu.make_async_copy(
            dy_ref.at[rows16(part), columns(z, y, c)],
            dyb.at[yi, z, rows16(part), pl.ds(512 * c, 512)],
            s_d1r.at[0],
        ).start()
    send_d1(0)

    def send_h1(k, carry):
        p = lax.rem(t + k, 16)
        remote(hs.at[p % 2, :, rows16(p // 2), :], h1.at[pl.ds(7 * t, 7)], s_h1s, s_h1r, d, p).start()
        return carry

    pltpu.make_async_copy(hs.at[lh, :, rows16(tg), :], h1.at[pl.ds(7 * t, 7)], s_h1r).start()
    lax.fori_loop(1, 16, send_h1, 0)

    def quant_group(g, carry):
        step = step_ref[pl.ds(g, 1), :]
        inverse = 1.0 / step

        def chunk(i, inner):
            rows = rows16(g * 16 + i)
            ratios = dw_ref[rows, :].astype(F32) * inverse
            clipped = jnp.clip(ratios, -8.0, 7.0)
            r = clipped - jnp.round(clipped)
            u = r * r
            s = r * horner(sin_series, u)
            c = horner(cos_series, u)
            levels = clipped - s * c * (1.0 / math.pi)
            slope = 2.0 * s * s
            slopes[rows, :] = slope
            extra[rows, :] = levels - ratios * slope
            qb[di, g, rows16(i), :] = (step * levels).astype(BF16)
            return inner

        lax.fori_loop(0, 16, chunk, 0)
        remote(qb.at[di, g], qb.at[di, g], s_qs.at[g], s_qr.at[g], d_c, t).start()
        return carry

    lax.fori_loop(0, 7, quant_group, 0)

    sibling = t + 1 - 2 * lh

    def d2_block(other, k):
        return dyb.at[yo if other else yi, :, rows16(lax.rem(part + 2 * k, 8)), :]

    def push_d2(other):
        await_bytes(dyb.at[0, :, 0:16, :], s_d1r.at[other])
        block = d2_block(other, 0)

        def send_d2(k, carry):
            remote(block, block, s_d2s, s_d2r.at[other, k], d, hi8 + lax.rem(part + 2 * k, 8)).start()
            return carry

        lax.fori_loop(1, 4, send_d2, 0)
        remote(block, block, s_d3s, s_d3r.at[other], d, sibling).start()

    def push_d3(other):
        def forward_d3(k, carry):
            block = d2_block(other, 4 - k)
            await_bytes(block, s_d2r.at[other, k])
            remote(block, block, s_d3s, s_d3r.at[other], d, sibling).start()
            return carry

        lax.fori_loop(1, 4, forward_d3, 0)

    push_d2(1)
    push_d2(0)
    push_d3(1)

    await_bytes(h1, s_h1r)

    def spread_h(a, carry):
        x = [h1[a * 4 + b].astype(F32) for b in range(4)]
        p0, p1, m0, m1 = x[0] + x[1], x[2] + x[3], x[0] - x[1], x[2] - x[3]
        mixf[0, a] = p0 + p1
        mixf[1, a] = m0 + m1
        mixf[2, a] = p0 - p1
        mixf[3, a] = m0 - m1
        return carry

    lax.fori_loop(0, 28, spread_h, 0)
    mix_paley(paley, mixf, h2, SCALE)

    def h_place(zz, ti):
        return hb.at[yi, ti % 2, :, pl.ds(pl.multiple_of(zz * 128 + (ti // 2) * 16, 16), 16), :]

    def send_h2(j, carry):
        zz, tt = peer64(j)
        remote(h2.at[pl.ds(7 * tt, 7)], h_place(z, t), s_h2s, s_h2r, zz * 4 + y, tt).start()
        return carry

    pltpu.make_async_copy(h2.at[pl.ds(7 * t, 7)], h_place(z, t), s_h2r).start()
    lax.fori_loop(1, 64, send_h2, 0)

    push_d3(0)
    await_bytes(dyb.at[0, :, 0:64, :], s_d3r.at[1])

    def product_g(which, g):
        total = dot(dyb[which, :, :, :512].reshape(512, 512), qb[0, g], 1, 1)
        return total + dot(dyb[which, :, :, 512:].reshape(512, 512), qb[1, g], 1, 1)

    def grad_group(g, carry):
        remote(qb.at[di, g], qb.at[do, g], s_qs.at[g], s_qr.at[g], d_c, t).wait_recv()
        theirs = product_g(yo, g).astype(BF16)
        gsend[g, 0] = theirs[:, :128]
        gsend[g, 1] = theirs[:, 128:]
        remote(gsend.at[g], gx.at[g], s_gxs.at[g], s_gxr.at[g], d_t, t).start()
        return carry

    lax.fori_loop(0, 7, grad_group, 0)
    await_bytes(dyb.at[0, :, 0:64, :], s_d3r.at[0])

    def own_group(g, carry):
        ours = product_g(yi, g).astype(BF16)
        gsum[0, g] = ours[:, :128]
        gsum[1, g] = ours[:, 128:]
        return carry

    lax.fori_loop(0, 7, own_group, 0)

    def add_group(g, carry):
        remote(gsend.at[g], gx.at[g], s_gxs.at[g], s_gxr.at[g], d_t, t).wait_recv()

        def chunk(i, inner):
            rows = pl.ds(pl.multiple_of(i * 64, 64), 64)
            for k in range(2):
                gsum[k, g, rows, :] = (gsum[k, g, rows, :].astype(F32) + gx[g, k, rows, :].astype(F32)).astype(BF16)
            return inner

        return lax.fori_loop(0, 8, chunk, carry)

    def push_g(chunk):
        q0, n = CHUNKS[chunk]

        def piece(zz, ti):
            return gsum.at[ti % 2, q0 : q0 + n, pl.ds(pl.multiple_of(zz * 128 + (ti // 2) * 16, 16), 16), :]

        place = gr.at[pl.ds(z * 112 + 7 * t + q0, n)]

        def send_gr(j, carry):
            zz, tt = peer64(j)
            remote(piece(zz, tt), place, s_grs, s_grr, zz * 4 + y, tt).start()
            return carry

        lax.fori_loop(q0, q0 + n, add_group, 0)
        pltpu.make_async_copy(piece(z, t), place, s_grr).start()
        lax.fori_loop(1, 64, send_gr, 0)

    push_g(0)

    def h_pass(q, which):
        return remote(hb.at[yi, :, q], hb.at[which, :, q], s_hxs.at[q], s_hxr.at[q], d_t, t)

    def forward_h(q, carry):
        h_pass(q, yi).start()
        return carry

    await_bytes(hb.at[yi], s_h2r)
    lax.fori_loop(0, 7, forward_h, 0)
    push_g(1)

    def product_d(q, half, c):
        cols = pl.ds(pl.multiple_of(c * 512, 512), 512)
        total = dot(hb[0, half, q], dyb[0, :, :, cols].reshape(512, 512), 0, 0)
        return total + dot(hb[1, half, q], dyb[1, :, :, cols].reshape(512, 512), 0, 0)

    def weight_group(q, carry):
        h_pass(q, yo).wait_recv()
        for half in range(2):
            dsend[q, 128 * half : 128 * half + 128, :] = product_d(q, half, do).astype(BF16)
        remote(dsend.at[q], dx.at[q], s_xs.at[q], s_xr.at[q], d_c, t).start()
        for half in range(2):
            wg_ref[pl.ds(pl.multiple_of(q * 256 + 128 * half, 128), 128), :] = product_d(q, half, di)
        return carry

    lax.fori_loop(0, 7, weight_group, 0)

    await_bytes(gr, s_grr)

    def spread_g(a, carry):
        x = []
        for b in range(4):
            total = gr[a * 4 + b].astype(F32)
            for zz in range(1, 4):
                total = total + gr[112 * zz + a * 4 + b].astype(F32)
            x.append(total)
        p0, p1, m0, m1 = x[0] + x[1], x[2] + x[3], x[0] - x[1], x[2] - x[3]
        mixf[0, a] = p0 + p1
        mixf[1, a] = m0 + m1
        mixf[2, a] = p0 - p1
        mixf[3, a] = m0 - m1
        return carry

    lax.fori_loop(0, 28, spread_g, 0)
    mix_paley(paley.T, mixf, gm, SCALE)

    def f_place(ti):
        return fr.at[ti % 2, :, rows16(ti // 2), :]

    def send_f(k, carry):
        p = lax.rem(t + k, 16)
        remote(gm.at[pl.ds(7 * p, 7)], f_place(t), s_fs, s_fr, d, p).start()
        return carry

    pltpu.make_async_copy(gm.at[pl.ds(7 * t, 7)], f_place(t), s_fr).start()
    lax.fori_loop(1, 16, send_f, 0)
    def weight_finish(q, carry):
        remote(dsend.at[q], dx.at[q], s_xs.at[q], s_xr.at[q], d_c, t).wait_recv()

        def chunk(i, acc):
            rows = rows16(q * 16 + i)
            total = wg_ref[rows, :] + dx[q, rows16(i), :].astype(F32)
            wg_ref[rows, :] = total * slopes[rows, :]
            return acc + total * extra[rows, :]

        acc = lax.fori_loop(0, 16, chunk, jnp.zeros((16, 512), F32))
        sg_ref[pl.ds(q, 1), :] = jnp.sum(acc, axis=0, keepdims=True) * (1.0 / math.sqrt(1792.0))
        return carry

    lax.fori_loop(0, 7, weight_finish, 0)
    await_bytes(fr, s_fr)

    await_bytes(h1.at[0:105], s_h1s)
    await_bytes(gr.at[0:441], s_h2s)
    await_bytes(gr.at[0:441], s_grs)
    await_bytes(gm.at[0:105], s_fs)
    await_bytes(dyb.at[0, 0, 0:112, :], s_d1s)
    await_bytes(dyb.at[:, :, 0:48, :], s_d2s)
    await_bytes(dyb.at[:, :, 0:64, :], s_d3s)

    def drain7(g, carry):
        remote(qb.at[di, g], qb.at[di, g], s_qs.at[g], s_qr.at[g], d_c, t).wait_send()
        remote(gsend.at[g], gx.at[g], s_gxs.at[g], s_gxr.at[g], d_t, t).wait_send()
        remote(dsend.at[g], dx.at[g], s_xs.at[g], s_xr.at[g], d_c, t).wait_send()
        h_pass(g, yi).wait_send()
        return carry

    lax.fori_loop(0, 7, drain7, 0)


def finish_kernel(
    gate_in, up_in, h256_in, fr_in, wg_in, sg_in, dgate_ref, dup_ref, wg_out, sg_out, gate, up, h256, fr, wg, sg, gh, sem
):
    bring = [
        pltpu.make_async_copy(src, dst, sem.at[i])
        for i, (src, dst) in enumerate(
            ((wg_in, wg), (fr_in, fr), (h256_in, h256), (gate_in, gate), (up_in, up), (sg_in, sg))
        )
    ]
    for copy in bring:
        copy.start()
    for copy in bring[1:]:
        copy.wait()
    sg_out[...] = sg[...]
    bring[0].wait()
    move = pltpu.make_async_copy(wg, wg_out, sem.at[0])
    move.start()
    for q in range(7):
        gh[...] = dot(fr[0, q], h256[:128, :], 1, 0) + dot(fr[1, q], h256[128:, :], 1, 0)
        cols = slice(256 * q, 256 * q + 256)

        def step(i, carry, cols=cols):
            rows = pl.ds(pl.multiple_of(i * 16, 16), 16)
            g = gate[rows, cols].astype(F32)
            u = up[rows, cols].astype(F32)
            sig = jax.nn.sigmoid(g)
            grad = gh[rows, :] * sig
            dup_ref[rows, cols] = (grad * g).astype(BF16)
            dgate_ref[rows, cols] = (grad * u * (1.0 + g * (1.0 - sig))).astype(BF16)
            return carry

        lax.fori_loop(0, 8, step, 0)
    move.wait()


def shards(d_out, gate_pre, up_pre, down_weight, step_size):
    h256 = jnp.asarray(sylvester(256), BF16)
    vmem = pl.BlockSpec(memory_space=pltpu.VMEM)
    dma = pltpu.SemaphoreType.DMA
    fr, weight, step = pl.pallas_call(
        kernel,
        out_shape=(
            jax.ShapeDtypeStruct((2, 7, 128, 128), BF16),
            jax.ShapeDtypeStruct((1792, 512), F32),
            jax.ShapeDtypeStruct((7, 512), F32),
        ),
        in_specs=[pl.BlockSpec(memory_space=pl.ANY)] + [vmem] * 5,
        out_specs=(vmem,) * 3,
        scratch_shapes=[
            pltpu.VMEM((128, 1792), BF16),
            pltpu.VMEM((2, 7, 128, 128), BF16),
            pltpu.VMEM((112, 16, 128), BF16),
            pltpu.VMEM((8, 28, 16, 128), F32),
            pltpu.VMEM((112, 16, 128), BF16),
            pltpu.VMEM((2, 2, 7, 512, 128), BF16),
            pltpu.VMEM((2, 4, 128, 1024), BF16),
            pltpu.VMEM((2, 7, 256, 512), BF16),
            pltpu.VMEM((1792, 512), F32),
            pltpu.VMEM((1792, 512), F32),
            pltpu.VMEM((7, 2, 512, 128), BF16),
            pltpu.VMEM((7, 2, 512, 128), BF16),
            pltpu.VMEM((2, 7, 512, 128), BF16),
            pltpu.VMEM((448, 16, 128), BF16),
            pltpu.VMEM((112, 16, 128), BF16),
            pltpu.VMEM((7, 256, 512), BF16),
            pltpu.VMEM((7, 256, 512), BF16),
            dma, dma,
            dma, dma,
            dma((7,)), dma((7,)),
            dma, dma((2,)),
            dma, dma((2, 4)),
            dma, dma((2,)),
            dma((7,)), dma((7,)),
            dma((7,)), dma((7,)),
            dma, dma,
            dma, dma,
            dma((7,)), dma((7,)),
        ],
        compiler_params=pltpu.CompilerParams(
            collective_id=0, has_side_effects=True, vmem_limit_bytes=58 * 1024 * 1024
        ),
        cost_estimate=pl.CostEstimate(flops=8_000_000_000, bytes_accessed=12_000_000, transcendentals=1_000_000),
    )(d_out, gate_pre, up_pre, down_weight, step_size, h256)
    anywhere = pl.BlockSpec(memory_space=pl.ANY)
    return pl.pallas_call(
        finish_kernel,
        out_shape=(
            jax.ShapeDtypeStruct((128, 1792), BF16),
            jax.ShapeDtypeStruct((128, 1792), BF16),
            jax.ShapeDtypeStruct((1792, 512), F32),
            jax.ShapeDtypeStruct((7, 512), F32),
        ),
        in_specs=[anywhere] * 6,
        out_specs=(vmem, vmem, anywhere, vmem),
        scratch_shapes=[
            pltpu.VMEM((128, 1792), BF16),
            pltpu.VMEM((128, 1792), BF16),
            pltpu.VMEM((256, 256), BF16),
            pltpu.VMEM((2, 7, 128, 128), BF16),
            pltpu.VMEM((1792, 512), F32),
            pltpu.VMEM((7, 512), F32),
            pltpu.VMEM((128, 256), F32),
            dma((6,)),
        ],
        compiler_params=pltpu.CompilerParams(vmem_limit_bytes=60 * 1024 * 1024),
        cost_estimate=pl.CostEstimate(flops=200_000_000, bytes_accessed=10_000_000, transcendentals=300_000),
    )(gate_pre, up_pre, h256, fr, weight, step)


def solution(mesh):
    return jax.shard_map(
        shards,
        mesh=mesh,
        in_specs=(
            P("dp", None),
            P("dp", "tensor"),
            P("dp", "tensor"),
            P("tensor", "dp"),
            P("tensor", "dp"),
        ),
        out_specs=(P("dp", "tensor"), P("dp", "tensor"), P("tensor", "dp"), P("tensor", "dp")),
        check_vma=False,
    )
```

```python
import math

import jax
import jax.numpy as jnp
import numpy as np
from jax import lax
from jax.experimental import pallas as pl
from jax.experimental.pallas import tpu as pltpu
from jax.sharding import PartitionSpec as P

FF = 28672
F32, BF16 = jnp.float32, jnp.bfloat16
MESH = pl.DeviceIdType.MESH
SCALE = 1.0 / math.sqrt(FF)
CHUNKS = ((0, 4), (4, 3))


def paley_matrix():
    digits_of = [(number % 3, number // 3 % 3, number // 9) for number in range(27)]
    lookup = {digits: number for number, digits in enumerate(digits_of)}

    def field_product(left_poly, right_poly):
        coeffs = [0, 0, 0, 0, 0]
        for left_pos in range(3):
            for right_pos in range(3):
                coeffs[left_pos + right_pos] += left_poly[left_pos] * right_poly[right_pos]
        for degree in (4, 3):
            excess = coeffs[degree]
            coeffs[degree] = 0
            coeffs[degree - 2] += excess
            coeffs[degree - 3] += 2 * excess
        return tuple((coefficient % 3 for coefficient in coeffs[:3]))

    squares_set = set((lookup[field_product(digits, digits)] for digits in digits_of[1:]))
    matrix_out = np.eye(28, dtype=np.float32)
    matrix_out[0, 1:] += 1.0
    matrix_out[1:, 0] -= 1.0
    for row_num in range(27):
        for col_num in range(27):
            if row_num != col_num:
                diff_poly = tuple(
                    (
                        (digits_of[row_num][position] - digits_of[col_num][position]) % 3
                        for position in range(3)
                    )
                )
                matrix_out[row_num + 1, col_num + 1] += (
                    1.0 if lookup[diff_poly] in squares_set else -1.0
                )
    return matrix_out


def sylvester(order_size):
    indices = np.arange(order_size)
    anded = indices[:, None] & indices[None, :]
    parity = np.zeros((order_size, order_size), np.int64)
    for bit_num in range(int(order_size).bit_length()):
        parity = parity + (anded >> bit_num & 1)
    return (1 - 2 * (parity % 2)).astype(np.float32)


def half_turn_series():
    points = 0.125 - 0.125 * np.cos((np.arange(64) + 0.5) * np.pi / 64)
    root = np.sqrt(points)
    a = np.polyfit(points, np.sin(np.pi * root) / root, 5)
    b = np.polyfit(points, np.cos(np.pi * root), 6)
    return [float(v) for v in a], [float(v) for v in b]


def horner(coefficients, u):
    total = coefficients[0] * u + coefficients[1]
    for c in coefficients[2:]:
        total = total * u + c
    return total


def dot(a, b, ca, cb):
    return lax.dot_general(a, b, (((ca,), (cb,)), ((), ())), preferred_element_type=F32)


def mix_paley(paley, src, dst, scale):
    def step(b, carry):
        for half in range(2):
            rows = slice(8 * half, 8 * half + 8)
            x = [src[b, a, rows, :] for a in range(28)]
            whole = x
            while len(whole) > 1:
                whole = [whole[i] + whole[i + 1] if i + 1 < len(whole) else whole[i] for i in range(0, len(whole), 2)]
            for c in range(28):
                negative = [x[a] for a in range(28) if paley[a, c] < 0]
                if negative:
                    less = negative[0]
                    for n in negative[1:]:
                        less = less + n
                    src[4 + b, c, rows, :] = (whole[0] - 2.0 * less) * scale
                else:
                    src[4 + b, c, rows, :] = whole[0] * scale
        for c in range(28):
            dst[c * 4 + b] = src[4 + b, c].astype(BF16)
        return carry

    lax.fori_loop(0, 4, step, 0)


def kernel(
    dy_ref, gate_in, up_in, dw_in, step_ref, h256_ref,
    dgate_out, dup_out, wg_out, sg_ref,
    gate_ref, up_ref, dw_ref, dgate, dup, up_factor, gate_factor, fr, gh, wg_ref, hid, hs, h1, mixf, h2, hb, dyb, qb, slopes, extra, gsend, gx, gsum, gr, gm, dsend, dx,
    s_h1s, s_h1r, s_h2s, s_h2r, s_hxs, s_hxr, s_d1s, s_d1r, s_d2s, s_d2r, s_d3s, s_d3r, s_qs, s_qr,
    s_gxs, s_gxr, s_grs, s_grr, s_fs, s_fr, s_xs, s_xr, s_w, s_in, s_gate, s_up,
):
    paley = paley_matrix()
    sin_series, cos_series = half_turn_series()
    d, t = lax.axis_index("dp"), lax.axis_index("tensor")
    z, y = d // 4, d % 4
    yi = y % 2
    yo = 1 - yi
    d_t = z * 4 + y + 1 - 2 * yi
    d_c = z * 4 + 3 - y
    di = y // 2
    do = 1 - di
    tg, lh = t // 2, t % 2
    part = t % 8
    hi8 = t - part

    def remote(src, dst, ss, rs, dev_d, dev_t):
        return pltpu.make_async_remote_copy(
            src_ref=src, dst_ref=dst, send_sem=ss, recv_sem=rs, device_id=(dev_d, dev_t), device_id_type=MESH
        )

    def await_bytes(ref, sem):
        pltpu.make_async_copy(ref, ref, sem).wait()

    def rows16(i):
        return pl.ds(pl.multiple_of(i * 16, 16), 16)

    def peer64(j):
        return lax.rem(z + j % 4, 4) , lax.rem(t + j // 4, 16)

    barrier = pltpu.get_barrier_semaphore()

    def greet(j, carry):
        zz, tt = peer64(j)
        pl.semaphore_signal(barrier, inc=1, device_id=(zz * 4 + y, tt), device_id_type=MESH)
        return carry

    lax.fori_loop(1, 64, greet, 0)
    for zz in range(4):
        pl.semaphore_signal(barrier, inc=1, device_id=(zz * 4 + y + 1 - 2 * yi, t), device_id_type=MESH)
    pl.semaphore_signal(barrier, inc=1, device_id=(d_c, t), device_id_type=MESH)

    fetch = [
        pltpu.make_async_copy(src, dst, s_in.at[i])
        for i, (src, dst) in enumerate(((gate_in, gate_ref), (up_in, up_ref), (dw_in, dw_ref)))
    ]
    for copy in fetch:
        copy.start()

    pl.semaphore_wait(barrier, 68)

    def columns(zz, yy, c):
        low = yy - (yy // 2) * (2 * yy - 3)
        return pl.ds(pl.multiple_of(512 * (zz * 4 + low + c * (3 - 2 * low)), 512), 512)

    def send_d1(other):
        yy = y - yi + (yo if other else yi)

        def step(j, carry):
            zz = lax.rem(z + j, 4)
            for c in range(2):
                remote(
                    dy_ref.at[rows16(part), columns(zz, yy, c)],
                    dyb.at[yi, z, rows16(part), pl.ds(512 * c, 512)],
                    s_d1s, s_d1r.at[other], zz * 4 + yy, t,
                ).start()
            return carry

        lax.fori_loop(1 - other, 4, step, 0)

    send_d1(1)
    for c in range(2):
        pltpu.make_async_copy(
            dy_ref.at[rows16(part), columns(z, y, c)],
            dyb.at[yi, z, rows16(part), pl.ds(512 * c, 512)],
            s_d1r.at[0],
        ).start()
    send_d1(0)

    fetch[0].wait()
    fetch[1].wait()

    def hidden_step(i, carry):
        rows = rows16(i)
        for q in range(7):
            cols = slice(256 * q, 256 * q + 256)
            g = gate_ref[rows, cols].astype(F32)
            u = up_ref[rows, cols].astype(F32)
            hid[rows, cols] = (g * jax.nn.sigmoid(g) * u).astype(BF16)
        return carry

    lax.fori_loop(0, 8, hidden_step, 0)
    for q in range(7):
        turned = dot(hid[:, 256 * q : 256 * q + 256], h256_ref[...], 1, 0).astype(BF16)
        hs[0, q] = turned[:, :128]
        hs[1, q] = turned[:, 128:]

    def send_h1(k, carry):
        p = lax.rem(t + k, 16)
        remote(hs.at[p % 2, :, rows16(p // 2), :], h1.at[pl.ds(7 * t, 7)], s_h1s, s_h1r, d, p).start()
        return carry

    pltpu.make_async_copy(hs.at[lh, :, rows16(tg), :], h1.at[pl.ds(7 * t, 7)], s_h1r).start()
    lax.fori_loop(1, 16, send_h1, 0)

    def quant_group(g, carry):
        step = step_ref[pl.ds(g, 1), :]
        inverse = 1.0 / step

        def chunk(i, inner):
            rows = rows16(g * 16 + i)
            ratios = dw_ref[rows, :].astype(F32) * inverse
            clipped = jnp.clip(ratios, -8.0, 7.0)
            r = clipped - jnp.round(clipped)
            u = r * r
            s = r * horner(sin_series, u)
            c = horner(cos_series, u)
            levels = clipped - s * c * (1.0 / math.pi)
            slope = 2.0 * s * s
            slopes[rows, :] = slope
            extra[rows, :] = levels - ratios * slope
            qb[di, g, rows16(i), :] = (step * levels).astype(BF16)
            return inner

        lax.fori_loop(0, 16, chunk, 0)
        remote(qb.at[di, g], qb.at[di, g], s_qs.at[g], s_qr.at[g], d_c, t).start()
        return carry

    fetch[2].wait()
    lax.fori_loop(0, 7, quant_group, 0)

    sibling = t + 1 - 2 * lh

    def d2_block(other, k):
        return dyb.at[yo if other else yi, :, rows16(lax.rem(part + 2 * k, 8)), :]

    def push_d2(other):
        await_bytes(dyb.at[0, :, 0:16, :], s_d1r.at[other])
        block = d2_block(other, 0)

        def send_d2(k, carry):
            remote(block, block, s_d2s, s_d2r.at[other, k], d, hi8 + lax.rem(part + 2 * k, 8)).start()
            return carry

        lax.fori_loop(1, 4, send_d2, 0)
        remote(block, block, s_d3s, s_d3r.at[other], d, sibling).start()

    def push_d3(other):
        def forward_d3(k, carry):
            block = d2_block(other, 4 - k)
            await_bytes(block, s_d2r.at[other, k])
            remote(block, block, s_d3s, s_d3r.at[other], d, sibling).start()
            return carry

        lax.fori_loop(1, 4, forward_d3, 0)

    push_d2(1)
    push_d2(0)
    push_d3(1)

    await_bytes(h1, s_h1r)

    def spread_h(a, carry):
        x = [h1[a * 4 + b].astype(F32) for b in range(4)]
        p0, p1, m0, m1 = x[0] + x[1], x[2] + x[3], x[0] - x[1], x[2] - x[3]
        mixf[0, a] = p0 + p1
        mixf[1, a] = m0 + m1
        mixf[2, a] = p0 - p1
        mixf[3, a] = m0 - m1
        return carry

    lax.fori_loop(0, 28, spread_h, 0)
    mix_paley(paley, mixf, h2, SCALE)

    def h_place(zz, ti):
        return hb.at[yi, ti % 2, :, pl.ds(pl.multiple_of(zz * 128 + (ti // 2) * 16, 16), 16), :]

    def send_h2(j, carry):
        zz, tt = peer64(j)
        remote(h2.at[pl.ds(7 * tt, 7)], h_place(z, t), s_h2s, s_h2r, zz * 4 + y, tt).start()
        return carry

    pltpu.make_async_copy(h2.at[pl.ds(7 * t, 7)], h_place(z, t), s_h2r).start()
    lax.fori_loop(1, 64, send_h2, 0)

    push_d3(0)
    await_bytes(dyb.at[0, :, 0:64, :], s_d3r.at[1])

    def product_g(which, g):
        total = dot(dyb[which, :, :, :512].reshape(512, 512), qb[0, g], 1, 1)
        return total + dot(dyb[which, :, :, 512:].reshape(512, 512), qb[1, g], 1, 1)

    def grad_group(g, carry):
        remote(qb.at[di, g], qb.at[do, g], s_qs.at[g], s_qr.at[g], d_c, t).wait_recv()
        theirs = product_g(yo, g).astype(BF16)
        gsend[g, 0] = theirs[:, :128]
        gsend[g, 1] = theirs[:, 128:]
        remote(gsend.at[g], gx.at[g], s_gxs.at[g], s_gxr.at[g], d_t, t).start()
        return carry

    lax.fori_loop(0, 7, grad_group, 0)
    await_bytes(dyb.at[0, :, 0:64, :], s_d3r.at[0])

    def own_group(g, carry):
        ours = product_g(yi, g).astype(BF16)
        gsum[0, g] = ours[:, :128]
        gsum[1, g] = ours[:, 128:]
        return carry

    lax.fori_loop(0, 7, own_group, 0)

    def factor_step(i, carry):
        rows = rows16(i)
        for q in range(7):
            cols = slice(256 * q, 256 * q + 256)
            g = gate_ref[rows, cols].astype(F32)
            u = up_ref[rows, cols].astype(F32)
            sig = jax.nn.sigmoid(g)
            up_factor[rows, cols] = g * sig
            gate_factor[rows, cols] = u * sig * (1.0 + g * (1.0 - sig))
        return carry

    lax.fori_loop(0, 8, factor_step, 0)

    def add_group(g, carry):
        remote(gsend.at[g], gx.at[g], s_gxs.at[g], s_gxr.at[g], d_t, t).wait_recv()

        def chunk(i, inner):
            rows = pl.ds(pl.multiple_of(i * 64, 64), 64)
            for k in range(2):
                gsum[k, g, rows, :] = (gsum[k, g, rows, :].astype(F32) + gx[g, k, rows, :].astype(F32)).astype(BF16)
            return inner

        return lax.fori_loop(0, 8, chunk, carry)

    def push_g(chunk):
        q0, n = CHUNKS[chunk]

        def piece(zz, ti):
            return gsum.at[ti % 2, q0 : q0 + n, pl.ds(pl.multiple_of(zz * 128 + (ti // 2) * 16, 16), 16), :]

        place = gr.at[pl.ds(z * 112 + 7 * t + q0, n)]

        def send_gr(j, carry):
            zz, tt = peer64(j)
            remote(piece(zz, tt), place, s_grs, s_grr, zz * 4 + y, tt).start()
            return carry

        lax.fori_loop(q0, q0 + n, add_group, 0)
        pltpu.make_async_copy(piece(z, t), place, s_grr).start()
        lax.fori_loop(1, 64, send_gr, 0)

    push_g(0)

    def h_pass(q, which):
        return remote(hb.at[yi, :, q], hb.at[which, :, q], s_hxs.at[q], s_hxr.at[q], d_t, t)

    def forward_h(q, carry):
        h_pass(q, yi).start()
        return carry

    await_bytes(hb.at[yi], s_h2r)
    lax.fori_loop(0, 7, forward_h, 0)
    push_g(1)

    def product_d(q, half, c):
        cols = pl.ds(pl.multiple_of(c * 512, 512), 512)
        total = dot(hb[0, half, q], dyb[0, :, :, cols].reshape(512, 512), 0, 0)
        return total + dot(hb[1, half, q], dyb[1, :, :, cols].reshape(512, 512), 0, 0)

    def weight_group(q, carry):
        h_pass(q, yo).wait_recv()
        for half in range(2):
            dsend[q, 128 * half : 128 * half + 128, :] = product_d(q, half, do).astype(BF16)
        remote(dsend.at[q], dx.at[q], s_xs.at[q], s_xr.at[q], d_c, t).start()
        for half in range(2):
            wg_ref[pl.ds(pl.multiple_of(q * 256 + 128 * half, 128), 128), :] = product_d(q, half, di)
        return carry

    lax.fori_loop(0, 6, weight_group, 0)

    await_bytes(gr, s_grr)

    def spread_g(a, carry):
        x = []
        for b in range(4):
            total = gr[a * 4 + b].astype(F32)
            for zz in range(1, 4):
                total = total + gr[112 * zz + a * 4 + b].astype(F32)
            x.append(total)
        p0, p1, m0, m1 = x[0] + x[1], x[2] + x[3], x[0] - x[1], x[2] - x[3]
        mixf[0, a] = p0 + p1
        mixf[1, a] = m0 + m1
        mixf[2, a] = p0 - p1
        mixf[3, a] = m0 - m1
        return carry

    lax.fori_loop(0, 28, spread_g, 0)
    mix_paley(paley.T, mixf, gm, SCALE)

    def f_place(ti):
        return fr.at[ti % 2, :, rows16(ti // 2), :]

    def send_f(k, carry):
        p = lax.rem(t + k, 16)
        remote(gm.at[pl.ds(7 * p, 7)], f_place(t), s_fs, s_fr, d, p).start()
        return carry

    pltpu.make_async_copy(gm.at[pl.ds(7 * t, 7)], f_place(t), s_fr).start()
    lax.fori_loop(1, 16, send_f, 0)
    lax.fori_loop(6, 7, weight_group, 0)
    def leave_w(q):
        rows = pl.ds(pl.multiple_of(q * 256, 256), 256)
        return pltpu.make_async_copy(wg_ref.at[rows, :], wg_out.at[rows, :], s_w.at[q])

    def weight_finish(q, carry):
        remote(dsend.at[q], dx.at[q], s_xs.at[q], s_xr.at[q], d_c, t).wait_recv()

        def chunk(i, acc):
            rows = rows16(q * 16 + i)
            total = wg_ref[rows, :] + dx[q, rows16(i), :].astype(F32)
            wg_ref[rows, :] = total * slopes[rows, :]
            return acc + total * extra[rows, :]

        acc = lax.fori_loop(0, 16, chunk, jnp.zeros((16, 512), F32))
        leave_w(q).start()
        sg_ref[pl.ds(q, 1), :] = jnp.sum(acc, axis=0, keepdims=True) * (1.0 / math.sqrt(1792.0))
        return carry

    lax.fori_loop(0, 7, weight_finish, 0)
    await_bytes(fr, s_fr)
    leave_g = []
    for q in range(7):
        gh[...] = dot(fr[0, q], h256_ref[:128, :], 1, 0) + dot(fr[1, q], h256_ref[128:, :], 1, 0)
        cols = slice(256 * q, 256 * q + 256)

        def finish_step(i, carry, cols=cols):
            rows = rows16(i)
            grad = gh[rows, :]
            dup[rows, cols] = (grad * up_factor[rows, cols]).astype(BF16)
            dgate[rows, cols] = (grad * gate_factor[rows, cols]).astype(BF16)
            return carry

        lax.fori_loop(0, 8, finish_step, 0, unroll=True)
        leave_g.append(pltpu.make_async_copy(dgate.at[:, cols], dgate_out.at[:, cols], s_gate.at[q]))
        leave_g.append(pltpu.make_async_copy(dup.at[:, cols], dup_out.at[:, cols], s_up.at[q]))
        leave_g[-1].start()
        leave_g[-2].start()

    await_bytes(h1.at[0:105], s_h1s)
    await_bytes(gr.at[0:441], s_h2s)
    await_bytes(gr.at[0:441], s_grs)
    await_bytes(gm.at[0:105], s_fs)
    await_bytes(dyb.at[0, 0, 0:112, :], s_d1s)
    await_bytes(dyb.at[:, :, 0:48, :], s_d2s)
    await_bytes(dyb.at[:, :, 0:64, :], s_d3s)

    def drain7(g, carry):
        remote(qb.at[di, g], qb.at[di, g], s_qs.at[g], s_qr.at[g], d_c, t).wait_send()
        remote(gsend.at[g], gx.at[g], s_gxs.at[g], s_gxr.at[g], d_t, t).wait_send()
        remote(dsend.at[g], dx.at[g], s_xs.at[g], s_xr.at[g], d_c, t).wait_send()
        h_pass(g, yi).wait_send()
        leave_w(g).wait()
        return carry

    lax.fori_loop(0, 7, drain7, 0)
    for copy in leave_g:
        copy.wait()


def copy_kernel(dgate_in, dup_in, wg_in, sg_in, dgate_out, dup_out, wg_out, sg_out, dgate, dup, wg, sg, s_in, s_out):
    routes = [(sg_in, sg, sg_out), (dgate_in, dgate, dgate_out), (dup_in, dup, dup_out)]
    for q in range(7):
        rows = pl.ds(256 * q, 256)
        routes.append((wg_in.at[rows, :], wg.at[rows, :], wg_out.at[rows, :]))
    bring = [pltpu.make_async_copy(src, via, s_in.at[i]) for i, (src, via, _) in enumerate(routes)]
    leave = [pltpu.make_async_copy(via, dst, s_out.at[i]) for i, (_, via, dst) in enumerate(routes)]
    for copy in bring:
        copy.start()
    for copy, then in zip(bring, leave):
        copy.wait()
        then.start()
    for copy in leave:
        copy.wait()


def shards(d_out, gate_pre, up_pre, down_weight, step_size):
    h256 = jnp.asarray(sylvester(256), BF16)
    vmem = pl.BlockSpec(memory_space=pltpu.VMEM)
    dma = pltpu.SemaphoreType.DMA
    anywhere = pl.BlockSpec(memory_space=pl.ANY)
    results = pl.pallas_call(
        kernel,
        out_shape=(
            jax.ShapeDtypeStruct((128, 1792), BF16),
            jax.ShapeDtypeStruct((128, 1792), BF16),
            jax.ShapeDtypeStruct((1792, 512), F32),
            jax.ShapeDtypeStruct((7, 512), F32),
        ),
        in_specs=[anywhere] * 4 + [vmem] * 2,
        out_specs=(anywhere, anywhere, anywhere, vmem),
        scratch_shapes=[
            pltpu.VMEM((128, 1792), BF16),
            pltpu.VMEM((128, 1792), BF16),
            pltpu.VMEM((1792, 512), BF16),
            pltpu.VMEM((128, 1792), BF16),
            pltpu.VMEM((128, 1792), BF16),
            pltpu.VMEM((128, 1792), F32),
            pltpu.VMEM((128, 1792), F32),
            pltpu.VMEM((2, 7, 128, 128), BF16),
            pltpu.VMEM((128, 256), F32),
            pltpu.VMEM((1792, 512), F32),
            pltpu.VMEM((128, 1792), BF16),
            pltpu.VMEM((2, 7, 128, 128), BF16),
            pltpu.VMEM((112, 16, 128), BF16),
            pltpu.VMEM((8, 28, 16, 128), F32),
            pltpu.VMEM((112, 16, 128), BF16),
            pltpu.VMEM((2, 2, 7, 512, 128), BF16),
            pltpu.VMEM((2, 4, 128, 1024), BF16),
            pltpu.VMEM((2, 7, 256, 512), BF16),
            pltpu.VMEM((1792, 512), F32),
            pltpu.VMEM((1792, 512), F32),
            pltpu.VMEM((7, 2, 512, 128), BF16),
            pltpu.VMEM((7, 2, 512, 128), BF16),
            pltpu.VMEM((2, 7, 512, 128), BF16),
            pltpu.VMEM((448, 16, 128), BF16),
            pltpu.VMEM((112, 16, 128), BF16),
            pltpu.VMEM((7, 256, 512), BF16),
            pltpu.VMEM((7, 256, 512), BF16),
            dma, dma,
            dma, dma,
            dma((7,)), dma((7,)),
            dma, dma((2,)),
            dma, dma((2, 4)),
            dma, dma((2,)),
            dma((7,)), dma((7,)),
            dma((7,)), dma((7,)),
            dma, dma,
            dma, dma,
            dma((7,)), dma((7,)),
            dma((7,)),
            dma((3,)), dma((7,)), dma((7,)),
        ],
        compiler_params=pltpu.CompilerParams(
            collective_id=0, has_side_effects=True, vmem_limit_bytes=58 * 1024 * 1024
        ),
        cost_estimate=pl.CostEstimate(flops=8_000_000_000, bytes_accessed=12_000_000, transcendentals=1_000_000),
    )(d_out, gate_pre, up_pre, down_weight, step_size, h256)
    return pl.pallas_call(
        copy_kernel,
        out_shape=(
            jax.ShapeDtypeStruct((128, 1792), BF16),
            jax.ShapeDtypeStruct((128, 1792), BF16),
            jax.ShapeDtypeStruct((1792, 512), F32),
            jax.ShapeDtypeStruct((7, 512), F32),
        ),
        in_specs=[anywhere] * 4,
        out_specs=(anywhere,) * 4,
        scratch_shapes=[
            pltpu.VMEM((128, 1792), BF16),
            pltpu.VMEM((128, 1792), BF16),
            pltpu.VMEM((1792, 512), F32),
            pltpu.VMEM((7, 512), F32),
            dma((10,)), dma((10,)),
        ],
        compiler_params=pltpu.CompilerParams(vmem_limit_bytes=60 * 1024 * 1024),
        cost_estimate=pl.CostEstimate(flops=0, bytes_accessed=10_000_000, transcendentals=0),
    )(*results)


def solution(mesh):
    return jax.shard_map(
        shards,
        mesh=mesh,
        in_specs=(
            P("dp", None),
            P("dp", "tensor"),
            P("dp", "tensor"),
            P("tensor", "dp"),
            P("tensor", "dp"),
        ),
        out_specs=(P("dp", "tensor"), P("dp", "tensor"), P("tensor", "dp"), P("tensor", "dp")),
        check_vma=False,
    )
```

```python
import math

import jax
import jax.numpy as jnp
import numpy as np
from jax import lax
from jax.experimental import pallas as pl
from jax.experimental.pallas import tpu as pltpu
from jax.sharding import PartitionSpec as P

FF = 28672
F32, BF16 = jnp.float32, jnp.bfloat16
MESH = pl.DeviceIdType.MESH
SCALE = 1.0 / math.sqrt(FF)
CHUNKS = ((0, 4), (4, 3))


def paley_matrix():
    digits_of = [(number % 3, number // 3 % 3, number // 9) for number in range(27)]
    lookup = {digits: number for number, digits in enumerate(digits_of)}

    def field_product(left_poly, right_poly):
        coeffs = [0, 0, 0, 0, 0]
        for left_pos in range(3):
            for right_pos in range(3):
                coeffs[left_pos + right_pos] += left_poly[left_pos] * right_poly[right_pos]
        for degree in (4, 3):
            excess = coeffs[degree]
            coeffs[degree] = 0
            coeffs[degree - 2] += excess
            coeffs[degree - 3] += 2 * excess
        return tuple((coefficient % 3 for coefficient in coeffs[:3]))

    squares_set = set((lookup[field_product(digits, digits)] for digits in digits_of[1:]))
    matrix_out = np.eye(28, dtype=np.float32)
    matrix_out[0, 1:] += 1.0
    matrix_out[1:, 0] -= 1.0
    for row_num in range(27):
        for col_num in range(27):
            if row_num != col_num:
                diff_poly = tuple(
                    (
                        (digits_of[row_num][position] - digits_of[col_num][position]) % 3
                        for position in range(3)
                    )
                )
                matrix_out[row_num + 1, col_num + 1] += (
                    1.0 if lookup[diff_poly] in squares_set else -1.0
                )
    return matrix_out


def sylvester(order_size):
    indices = np.arange(order_size)
    anded = indices[:, None] & indices[None, :]
    parity = np.zeros((order_size, order_size), np.int64)
    for bit_num in range(int(order_size).bit_length()):
        parity = parity + (anded >> bit_num & 1)
    return (1 - 2 * (parity % 2)).astype(np.float32)


def half_turn_series():
    points = 0.125 - 0.125 * np.cos((np.arange(64) + 0.5) * np.pi / 64)
    root = np.sqrt(points)
    a = np.polyfit(points, np.sin(np.pi * root) / root, 5)
    b = np.polyfit(points, np.cos(np.pi * root), 6)
    return [float(v) for v in a], [float(v) for v in b]


def horner(coefficients, u):
    total = coefficients[0] * u + coefficients[1]
    for c in coefficients[2:]:
        total = total * u + c
    return total


def dot(a, b, ca, cb):
    return lax.dot_general(a, b, (((ca,), (cb,)), ((), ())), preferred_element_type=F32)


def mix_paley(paley, src, dst, scale):
    def step(b, carry):
        for half in range(2):
            rows = slice(8 * half, 8 * half + 8)
            x = [src[b, a, rows, :] for a in range(28)]
            whole = x
            while len(whole) > 1:
                whole = [whole[i] + whole[i + 1] if i + 1 < len(whole) else whole[i] for i in range(0, len(whole), 2)]
            for c in range(28):
                negative = [x[a] for a in range(28) if paley[a, c] < 0]
                if negative:
                    less = negative[0]
                    for n in negative[1:]:
                        less = less + n
                    src[4 + b, c, rows, :] = (whole[0] - 2.0 * less) * scale
                else:
                    src[4 + b, c, rows, :] = whole[0] * scale
        for c in range(28):
            dst[c * 4 + b] = src[4 + b, c].astype(BF16)
        return carry

    lax.fori_loop(0, 4, step, 0)


def kernel(
    dy_ref, gate_in, up_in, dw_in, step_in, h256_in,
    dgate_out, dup_out, wg_out, sg_ref,
    gate_ref, up_ref, dw_ref, step_ref, h256_ref, dgate, dup, up_factor, gate_factor, fr, gh, wg_ref, hid, hs, h1, mixf, h2, hb, dyb, qb, slopes, extra, gsend, gx, gsum, gr, gm, dsend, dx,
    s_h1s, s_h1r, s_h2s, s_h2r, s_hxs, s_hxr, s_d1s, s_d1r, s_d2s, s_d2r, s_d3s, s_d3r, s_qs, s_qr,
    s_gxs, s_gxr, s_grs, s_grr, s_fs, s_fr, s_xs, s_xr, s_w, s_in, s_gate, s_up,
):
    paley = paley_matrix()
    sin_series, cos_series = half_turn_series()
    d, t = lax.axis_index("dp"), lax.axis_index("tensor")
    z, y = d // 4, d % 4
    yi = y % 2
    yo = 1 - yi
    d_t = z * 4 + y + 1 - 2 * yi
    d_c = z * 4 + 3 - y
    di = y // 2
    do = 1 - di
    tg, lh = t // 2, t % 2
    part = t % 8
    hi8 = t - part

    def remote(src, dst, ss, rs, dev_d, dev_t):
        return pltpu.make_async_remote_copy(
            src_ref=src, dst_ref=dst, send_sem=ss, recv_sem=rs, device_id=(dev_d, dev_t), device_id_type=MESH
        )

    def await_bytes(ref, sem):
        pltpu.make_async_copy(ref, ref, sem).wait()

    def rows16(i):
        return pl.ds(pl.multiple_of(i * 16, 16), 16)

    def peer64(j):
        return lax.rem(z + j % 4, 4) , lax.rem(t + 9 * (j // 4), 16)

    barrier = pltpu.get_barrier_semaphore()

    def greet(j, carry):
        zz, tt = peer64(j)
        pl.semaphore_signal(barrier, inc=1, device_id=(zz * 4 + y, tt), device_id_type=MESH)
        return carry

    lax.fori_loop(1, 64, greet, 0)
    for zz in range(4):
        pl.semaphore_signal(barrier, inc=1, device_id=(zz * 4 + y + 1 - 2 * yi, t), device_id_type=MESH)
    pl.semaphore_signal(barrier, inc=1, device_id=(d_c, t), device_id_type=MESH)

    fetch = [
        pltpu.make_async_copy(src, dst, s_in.at[i])
        for i, (src, dst) in enumerate(
            ((gate_in, gate_ref), (up_in, up_ref), (h256_in, h256_ref), (dw_in, dw_ref), (step_in, step_ref))
        )
    ]
    for copy in fetch:
        copy.start()

    pl.semaphore_wait(barrier, 68)

    def columns(zz, yy, c):
        low = yy - (yy // 2) * (2 * yy - 3)
        return pl.ds(pl.multiple_of(512 * (zz * 4 + low + c * (3 - 2 * low)), 512), 512)

    def send_d1(other):
        yy = y - yi + (yo if other else yi)

        def step(j, carry):
            zz = lax.rem(z + j, 4)
            for c in range(2):
                remote(
                    dy_ref.at[rows16(part), columns(zz, yy, c)],
                    dyb.at[yi, z, rows16(part), pl.ds(512 * c, 512)],
                    s_d1s, s_d1r.at[other], zz * 4 + yy, t,
                ).start()
            return carry

        lax.fori_loop(1 - other, 4, step, 0)

    send_d1(1)
    for c in range(2):
        pltpu.make_async_copy(
            dy_ref.at[rows16(part), columns(z, y, c)],
            dyb.at[yi, z, rows16(part), pl.ds(512 * c, 512)],
            s_d1r.at[0],
        ).start()
    send_d1(0)

    for copy in fetch[:3]:
        copy.wait()

    def hidden_step(i, carry):
        rows = rows16(i)
        for q in range(7):
            cols = slice(256 * q, 256 * q + 256)
            g = gate_ref[rows, cols].astype(F32)
            u = up_ref[rows, cols].astype(F32)
            hid[rows, cols] = (g * jax.nn.sigmoid(g) * u).astype(BF16)
        return carry

    lax.fori_loop(0, 8, hidden_step, 0)
    for q in range(7):
        turned = dot(hid[:, 256 * q : 256 * q + 256], h256_ref[...], 1, 0).astype(BF16)
        hs[0, q] = turned[:, :128]
        hs[1, q] = turned[:, 128:]

    def send_h1(k, carry):
        p = lax.rem(t + 9 * k, 16)
        remote(hs.at[p % 2, :, rows16(p // 2), :], h1.at[pl.ds(7 * t, 7)], s_h1s, s_h1r, d, p).start()
        return carry

    pltpu.make_async_copy(hs.at[lh, :, rows16(tg), :], h1.at[pl.ds(7 * t, 7)], s_h1r).start()
    lax.fori_loop(1, 16, send_h1, 0)

    def quant_group(g, carry):
        step = step_ref[pl.ds(g, 1), :]
        inverse = 1.0 / step

        def chunk(i, inner):
            rows = rows16(g * 16 + i)
            ratios = dw_ref[rows, :].astype(F32) * inverse
            clipped = jnp.clip(ratios, -8.0, 7.0)
            r = clipped - jnp.round(clipped)
            u = r * r
            s = r * horner(sin_series, u)
            c = horner(cos_series, u)
            levels = clipped - s * c * (1.0 / math.pi)
            slope = 2.0 * s * s
            slopes[rows, :] = slope
            extra[rows, :] = levels - ratios * slope
            qb[di, g, rows16(i), :] = (step * levels).astype(BF16)
            return inner

        lax.fori_loop(0, 16, chunk, 0)
        remote(qb.at[di, g], qb.at[di, g], s_qs.at[g], s_qr.at[g], d_c, t).start()
        return carry

    fetch[3].wait()
    fetch[4].wait()
    lax.fori_loop(0, 7, quant_group, 0)

    sibling = t + 1 - 2 * lh

    def d2_block(other, k):
        return dyb.at[yo if other else yi, :, rows16(lax.rem(part + 2 * k, 8)), :]

    def push_d2(other):
        await_bytes(dyb.at[0, :, 0:16, :], s_d1r.at[other])
        block = d2_block(other, 0)

        def send_d2(k, carry):
            remote(block, block, s_d2s, s_d2r.at[other, k], d, hi8 + lax.rem(part + 2 * k, 8)).start()
            return carry

        lax.fori_loop(1, 4, send_d2, 0)
        remote(block, block, s_d3s, s_d3r.at[other], d, sibling).start()

    def push_d3(other):
        def forward_d3(k, carry):
            block = d2_block(other, 4 - k)
            await_bytes(block, s_d2r.at[other, k])
            remote(block, block, s_d3s, s_d3r.at[other], d, sibling).start()
            return carry

        lax.fori_loop(1, 4, forward_d3, 0)

    push_d2(1)
    push_d2(0)
    push_d3(1)

    await_bytes(h1, s_h1r)

    def spread_h(a, carry):
        x = [h1[a * 4 + b].astype(F32) for b in range(4)]
        p0, p1, m0, m1 = x[0] + x[1], x[2] + x[3], x[0] - x[1], x[2] - x[3]
        mixf[0, a] = p0 + p1
        mixf[1, a] = m0 + m1
        mixf[2, a] = p0 - p1
        mixf[3, a] = m0 - m1
        return carry

    lax.fori_loop(0, 28, spread_h, 0)
    mix_paley(paley, mixf, h2, SCALE)

    def h_place(zz, ti):
        return hb.at[yi, ti % 2, :, pl.ds(pl.multiple_of(zz * 128 + (ti // 2) * 16, 16), 16), :]

    def send_h2(j, carry):
        zz, tt = peer64(j)
        remote(h2.at[pl.ds(7 * tt, 7)], h_place(z, t), s_h2s, s_h2r, zz * 4 + y, tt).start()
        return carry

    pltpu.make_async_copy(h2.at[pl.ds(7 * t, 7)], h_place(z, t), s_h2r).start()
    lax.fori_loop(1, 64, send_h2, 0)

    push_d3(0)
    await_bytes(dyb.at[0, :, 0:64, :], s_d3r.at[1])

    def product_g(which, g):
        total = dot(dyb[which, :, :, :512].reshape(512, 512), qb[0, g], 1, 1)
        return total + dot(dyb[which, :, :, 512:].reshape(512, 512), qb[1, g], 1, 1)

    def grad_group(g, carry):
        remote(qb.at[di, g], qb.at[do, g], s_qs.at[g], s_qr.at[g], d_c, t).wait_recv()
        theirs = product_g(yo, g).astype(BF16)
        gsend[g, 0] = theirs[:, :128]
        gsend[g, 1] = theirs[:, 128:]
        remote(gsend.at[g], gx.at[g], s_gxs.at[g], s_gxr.at[g], d_t, t).start()
        return carry

    lax.fori_loop(0, 7, grad_group, 0)
    await_bytes(dyb.at[0, :, 0:64, :], s_d3r.at[0])

    def own_group(g, carry):
        ours = product_g(yi, g).astype(BF16)
        gsum[0, g] = ours[:, :128]
        gsum[1, g] = ours[:, 128:]
        return carry

    lax.fori_loop(0, 7, own_group, 0)

    def factor_step(i, carry):
        rows = rows16(i)
        for q in range(7):
            cols = slice(256 * q, 256 * q + 256)
            g = gate_ref[rows, cols].astype(F32)
            u = up_ref[rows, cols].astype(F32)
            sig = jax.nn.sigmoid(g)
            up_factor[rows, cols] = g * sig
            gate_factor[rows, cols] = u * sig * (1.0 + g * (1.0 - sig))
        return carry

    lax.fori_loop(0, 8, factor_step, 0)

    def add_group(g, carry):
        remote(gsend.at[g], gx.at[g], s_gxs.at[g], s_gxr.at[g], d_t, t).wait_recv()

        def chunk(i, inner):
            rows = pl.ds(pl.multiple_of(i * 64, 64), 64)
            for k in range(2):
                gsum[k, g, rows, :] = (gsum[k, g, rows, :].astype(F32) + gx[g, k, rows, :].astype(F32)).astype(BF16)
            return inner

        return lax.fori_loop(0, 8, chunk, carry)

    def push_g(chunk):
        q0, n = CHUNKS[chunk]

        def piece(zz, ti):
            return gsum.at[ti % 2, q0 : q0 + n, pl.ds(pl.multiple_of(zz * 128 + (ti // 2) * 16, 16), 16), :]

        place = gr.at[pl.ds(z * 112 + 7 * t + q0, n)]

        def send_gr(j, carry):
            zz, tt = peer64(j)
            remote(piece(zz, tt), place, s_grs, s_grr, zz * 4 + y, tt).start()
            return carry

        lax.fori_loop(q0, q0 + n, add_group, 0)
        pltpu.make_async_copy(piece(z, t), place, s_grr).start()
        lax.fori_loop(1, 64, send_gr, 0)

    push_g(0)

    def h_pass(q, which):
        return remote(hb.at[yi, :, q], hb.at[which, :, q], s_hxs.at[q], s_hxr.at[q], d_t, t)

    def forward_h(q, carry):
        h_pass(q, yi).start()
        return carry

    await_bytes(hb.at[yi], s_h2r)
    lax.fori_loop(0, 7, forward_h, 0)
    push_g(1)

    def product_d(q, half, c):
        cols = pl.ds(pl.multiple_of(c * 512, 512), 512)
        total = dot(hb[0, half, q], dyb[0, :, :, cols].reshape(512, 512), 0, 0)
        return total + dot(hb[1, half, q], dyb[1, :, :, cols].reshape(512, 512), 0, 0)

    def weight_group(q, carry):
        h_pass(q, yo).wait_recv()
        for half in range(2):
            dsend[q, 128 * half : 128 * half + 128, :] = product_d(q, half, do).astype(BF16)
        remote(dsend.at[q], dx.at[q], s_xs.at[q], s_xr.at[q], d_c, t).start()
        for half in range(2):
            wg_ref[pl.ds(pl.multiple_of(q * 256 + 128 * half, 128), 128), :] = product_d(q, half, di)
        return carry

    lax.fori_loop(0, 5, weight_group, 0)

    await_bytes(gr, s_grr)

    def spread_g(a, carry):
        x = []
        for b in range(4):
            total = gr[a * 4 + b].astype(F32)
            for zz in range(1, 4):
                total = total + gr[112 * zz + a * 4 + b].astype(F32)
            x.append(total)
        p0, p1, m0, m1 = x[0] + x[1], x[2] + x[3], x[0] - x[1], x[2] - x[3]
        mixf[0, a] = p0 + p1
        mixf[1, a] = m0 + m1
        mixf[2, a] = p0 - p1
        mixf[3, a] = m0 - m1
        return carry

    lax.fori_loop(0, 28, spread_g, 0)
    mix_paley(paley.T, mixf, gm, SCALE)

    def f_place(ti):
        return fr.at[ti % 2, :, rows16(ti // 2), :]

    def send_f(k, carry):
        p = lax.rem(t + 9 * k, 16)
        remote(gm.at[pl.ds(7 * p, 7)], f_place(t), s_fs, s_fr, d, p).start()
        return carry

    pltpu.make_async_copy(gm.at[pl.ds(7 * t, 7)], f_place(t), s_fr).start()
    lax.fori_loop(1, 16, send_f, 0)
    lax.fori_loop(5, 7, weight_group, 0)
    def leave_w(q):
        rows = pl.ds(pl.multiple_of(q * 256, 256), 256)
        return pltpu.make_async_copy(wg_ref.at[rows, :], wg_out.at[rows, :], s_w.at[q])

    def weight_finish(q, carry):
        remote(dsend.at[q], dx.at[q], s_xs.at[q], s_xr.at[q], d_c, t).wait_recv()

        def chunk(i, acc):
            rows = rows16(q * 16 + i)
            total = wg_ref[rows, :] + dx[q, rows16(i), :].astype(F32)
            wg_ref[rows, :] = total * slopes[rows, :]
            return acc + total * extra[rows, :]

        acc = lax.fori_loop(0, 16, chunk, jnp.zeros((16, 512), F32))
        leave_w(q).start()
        sg_ref[pl.ds(q, 1), :] = jnp.sum(acc, axis=0, keepdims=True) * (1.0 / math.sqrt(1792.0))
        return carry

    lax.fori_loop(0, 7, weight_finish, 0)
    await_bytes(fr, s_fr)
    leave_g = []
    for q in range(7):
        gh[...] = dot(fr[0, q], h256_ref[:128, :], 1, 0) + dot(fr[1, q], h256_ref[128:, :], 1, 0)
        cols = slice(256 * q, 256 * q + 256)

        def finish_step(i, carry, cols=cols):
            rows = rows16(i)
            grad = gh[rows, :]
            dup[rows, cols] = (grad * up_factor[rows, cols]).astype(BF16)
            dgate[rows, cols] = (grad * gate_factor[rows, cols]).astype(BF16)
            return carry

        lax.fori_loop(0, 8, finish_step, 0, unroll=True)
        leave_g.append(pltpu.make_async_copy(dgate.at[:, cols], dgate_out.at[:, cols], s_gate.at[q]))
        leave_g.append(pltpu.make_async_copy(dup.at[:, cols], dup_out.at[:, cols], s_up.at[q]))
        leave_g[-1].start()
        leave_g[-2].start()

    await_bytes(h1.at[0:105], s_h1s)
    await_bytes(gr.at[0:441], s_h2s)
    await_bytes(gr.at[0:441], s_grs)
    await_bytes(gm.at[0:105], s_fs)
    await_bytes(dyb.at[0, 0, 0:112, :], s_d1s)
    await_bytes(dyb.at[:, :, 0:48, :], s_d2s)
    await_bytes(dyb.at[:, :, 0:64, :], s_d3s)

    def drain7(g, carry):
        remote(qb.at[di, g], qb.at[di, g], s_qs.at[g], s_qr.at[g], d_c, t).wait_send()
        remote(gsend.at[g], gx.at[g], s_gxs.at[g], s_gxr.at[g], d_t, t).wait_send()
        remote(dsend.at[g], dx.at[g], s_xs.at[g], s_xr.at[g], d_c, t).wait_send()
        h_pass(g, yi).wait_send()
        leave_w(g).wait()
        return carry

    lax.fori_loop(0, 7, drain7, 0)
    for copy in leave_g:
        copy.wait()


def copy_kernel(dgate_in, dup_in, wg_in, sg_in, dgate_out, dup_out, wg_out, sg_out, dgate, dup, wg, sg, s_in, s_out):
    routes = [(sg_in, sg, sg_out), (dgate_in, dgate, dgate_out), (dup_in, dup, dup_out)]
    for q in range(7):
        rows = pl.ds(256 * q, 256)
        routes.append((wg_in.at[rows, :], wg.at[rows, :], wg_out.at[rows, :]))
    bring = [pltpu.make_async_copy(src, via, s_in.at[i]) for i, (src, via, _) in enumerate(routes)]
    leave = [pltpu.make_async_copy(via, dst, s_out.at[i]) for i, (_, via, dst) in enumerate(routes)]
    for copy in bring:
        copy.start()
    for copy, then in zip(bring, leave):
        copy.wait()
        then.start()
    for copy in leave:
        copy.wait()


def shards(d_out, gate_pre, up_pre, down_weight, step_size):
    h256 = jnp.asarray(sylvester(256), BF16)
    vmem = pl.BlockSpec(memory_space=pltpu.VMEM)
    dma = pltpu.SemaphoreType.DMA
    anywhere = pl.BlockSpec(memory_space=pl.ANY)
    results = pl.pallas_call(
        kernel,
        out_shape=(
            jax.ShapeDtypeStruct((128, 1792), BF16),
            jax.ShapeDtypeStruct((128, 1792), BF16),
            jax.ShapeDtypeStruct((1792, 512), F32),
            jax.ShapeDtypeStruct((7, 512), F32),
        ),
        in_specs=[anywhere] * 6,
        out_specs=(anywhere, anywhere, anywhere, vmem),
        scratch_shapes=[
            pltpu.VMEM((128, 1792), BF16),
            pltpu.VMEM((128, 1792), BF16),
            pltpu.VMEM((1792, 512), BF16),
            pltpu.VMEM((7, 512), F32),
            pltpu.VMEM((256, 256), BF16),
            pltpu.VMEM((128, 1792), BF16),
            pltpu.VMEM((128, 1792), BF16),
            pltpu.VMEM((128, 1792), F32),
            pltpu.VMEM((128, 1792), F32),
            pltpu.VMEM((2, 7, 128, 128), BF16),
            pltpu.VMEM((128, 256), F32),
            pltpu.VMEM((1792, 512), F32),
            pltpu.VMEM((128, 1792), BF16),
            pltpu.VMEM((2, 7, 128, 128), BF16),
            pltpu.VMEM((112, 16, 128), BF16),
            pltpu.VMEM((8, 28, 16, 128), F32),
            pltpu.VMEM((112, 16, 128), BF16),
            pltpu.VMEM((2, 2, 7, 512, 128), BF16),
            pltpu.VMEM((2, 4, 128, 1024), BF16),
            pltpu.VMEM((2, 7, 256, 512), BF16),
            pltpu.VMEM((1792, 512), F32),
            pltpu.VMEM((1792, 512), F32),
            pltpu.VMEM((7, 2, 512, 128), BF16),
            pltpu.VMEM((7, 2, 512, 128), BF16),
            pltpu.VMEM((2, 7, 512, 128), BF16),
            pltpu.VMEM((448, 16, 128), BF16),
            pltpu.VMEM((112, 16, 128), BF16),
            pltpu.VMEM((7, 256, 512), BF16),
            pltpu.VMEM((7, 256, 512), BF16),
            dma, dma,
            dma, dma,
            dma((7,)), dma((7,)),
            dma, dma((2,)),
            dma, dma((2, 4)),
            dma, dma((2,)),
            dma((7,)), dma((7,)),
            dma((7,)), dma((7,)),
            dma, dma,
            dma, dma,
            dma((7,)), dma((7,)),
            dma((7,)),
            dma((5,)), dma((7,)), dma((7,)),
        ],
        compiler_params=pltpu.CompilerParams(
            collective_id=0, has_side_effects=True, vmem_limit_bytes=58 * 1024 * 1024
        ),
        cost_estimate=pl.CostEstimate(flops=8_000_000_000, bytes_accessed=12_000_000, transcendentals=1_000_000),
    )(d_out, gate_pre, up_pre, down_weight, step_size, h256)
    return pl.pallas_call(
        copy_kernel,
        out_shape=(
            jax.ShapeDtypeStruct((128, 1792), BF16),
            jax.ShapeDtypeStruct((128, 1792), BF16),
            jax.ShapeDtypeStruct((1792, 512), F32),
            jax.ShapeDtypeStruct((7, 512), F32),
        ),
        in_specs=[anywhere] * 4,
        out_specs=(anywhere,) * 4,
        scratch_shapes=[
            pltpu.VMEM((128, 1792), BF16),
            pltpu.VMEM((128, 1792), BF16),
            pltpu.VMEM((1792, 512), F32),
            pltpu.VMEM((7, 512), F32),
            dma((10,)), dma((10,)),
        ],
        compiler_params=pltpu.CompilerParams(vmem_limit_bytes=60 * 1024 * 1024),
        cost_estimate=pl.CostEstimate(flops=0, bytes_accessed=10_000_000, transcendentals=0),
    )(*results)


def solution(mesh):
    return jax.shard_map(
        shards,
        mesh=mesh,
        in_specs=(
            P("dp", None),
            P("dp", "tensor"),
            P("dp", "tensor"),
            P("tensor", "dp"),
            P("tensor", "dp"),
        ),
        out_specs=(P("dp", "tensor"), P("dp", "tensor"), P("tensor", "dp"), P("tensor", "dp")),
        check_vma=False,
    )
```

```python
import math

import jax
import jax.numpy as jnp
import numpy as np
from jax import lax
from jax.experimental import pallas as pl
from jax.experimental.pallas import tpu as pltpu
from jax.sharding import PartitionSpec as P

FF = 28672
F32, BF16 = jnp.float32, jnp.bfloat16
MESH = pl.DeviceIdType.MESH
SCALE = 1.0 / math.sqrt(FF)
CHUNKS = ((0, 4), (4, 3))


def paley_matrix():
    digits_of = [(number % 3, number // 3 % 3, number // 9) for number in range(27)]
    lookup = {digits: number for number, digits in enumerate(digits_of)}

    def field_product(left_poly, right_poly):
        coeffs = [0, 0, 0, 0, 0]
        for left_pos in range(3):
            for right_pos in range(3):
                coeffs[left_pos + right_pos] += left_poly[left_pos] * right_poly[right_pos]
        for degree in (4, 3):
            excess = coeffs[degree]
            coeffs[degree] = 0
            coeffs[degree - 2] += excess
            coeffs[degree - 3] += 2 * excess
        return tuple((coefficient % 3 for coefficient in coeffs[:3]))

    squares_set = set((lookup[field_product(digits, digits)] for digits in digits_of[1:]))
    matrix_out = np.eye(28, dtype=np.float32)
    matrix_out[0, 1:] += 1.0
    matrix_out[1:, 0] -= 1.0
    for row_num in range(27):
        for col_num in range(27):
            if row_num != col_num:
                diff_poly = tuple(
                    (
                        (digits_of[row_num][position] - digits_of[col_num][position]) % 3
                        for position in range(3)
                    )
                )
                matrix_out[row_num + 1, col_num + 1] += (
                    1.0 if lookup[diff_poly] in squares_set else -1.0
                )
    return matrix_out


def sylvester(order_size):
    indices = np.arange(order_size)
    anded = indices[:, None] & indices[None, :]
    parity = np.zeros((order_size, order_size), np.int64)
    for bit_num in range(int(order_size).bit_length()):
        parity = parity + (anded >> bit_num & 1)
    return (1 - 2 * (parity % 2)).astype(np.float32)


def half_turn_series():
    points = 0.125 - 0.125 * np.cos((np.arange(64) + 0.5) * np.pi / 64)
    root = np.sqrt(points)
    a = np.polyfit(points, np.sin(np.pi * root) / root, 5)
    b = np.polyfit(points, np.cos(np.pi * root), 6)
    return [float(v) for v in a], [float(v) for v in b]


def horner(coefficients, u):
    total = coefficients[0] * u + coefficients[1]
    for c in coefficients[2:]:
        total = total * u + c
    return total


def dot(a, b, ca, cb):
    return lax.dot_general(a, b, (((ca,), (cb,)), ((), ())), preferred_element_type=F32)


def mix_paley(paley, src, dst, scale):
    def step(b, carry):
        for half in range(2):
            rows = slice(8 * half, 8 * half + 8)
            x = [src[b, a, rows, :] for a in range(28)]
            whole = x
            while len(whole) > 1:
                whole = [whole[i] + whole[i + 1] if i + 1 < len(whole) else whole[i] for i in range(0, len(whole), 2)]
            for c in range(28):
                negative = [x[a] for a in range(28) if paley[a, c] < 0]
                if negative:
                    less = negative[0]
                    for n in negative[1:]:
                        less = less + n
                    src[4 + b, c, rows, :] = (whole[0] - 2.0 * less) * scale
                else:
                    src[4 + b, c, rows, :] = whole[0] * scale
        for c in range(28):
            dst[c * 4 + b] = src[4 + b, c].astype(BF16)
        return carry

    lax.fori_loop(0, 4, step, 0)


def kernel(
    dy_ref, gate_in, up_in, dw_in, step_in, h256_in,
    dgate_out, dup_out, wg_out, sg_ref,
    gate_ref, up_ref, dw_ref, step_ref, h256_ref, dgate, dup, up_factor, gate_factor, fr, gh, wg_ref, hid, hs, h1, mixf, h2, hb, dyb, qb, slopes, extra, gsend, gx, gsum, gr, gm, dsend, dx,
    s_h1s, s_h1r, s_h2s, s_h2r, s_hxs, s_hxr, s_d1s, s_d1r, s_d2s, s_d2r, s_d3s, s_d3r, s_qs, s_qr,
    s_gxs, s_gxr, s_grs, s_grr, s_fs, s_fr, s_xs, s_xr, s_w, s_in, s_gate, s_up,
):
    paley = paley_matrix()
    sin_series, cos_series = half_turn_series()
    d, t = lax.axis_index("dp"), lax.axis_index("tensor")
    z, y = d // 4, d % 4
    yi = y % 2
    yo = 1 - yi
    d_t = z * 4 + y + 1 - 2 * yi
    d_c = z * 4 + 3 - y
    di = y // 2
    do = 1 - di
    tg, lh = t // 2, t % 2
    part = t % 8
    hi8 = t - part

    def remote(src, dst, ss, rs, dev_d, dev_t):
        return pltpu.make_async_remote_copy(
            src_ref=src, dst_ref=dst, send_sem=ss, recv_sem=rs, device_id=(dev_d, dev_t), device_id_type=MESH
        )

    def await_bytes(ref, sem):
        pltpu.make_async_copy(ref, ref, sem).wait()

    def rows16(i):
        return pl.ds(pl.multiple_of(i * 16, 16), 16)

    def peer64(j):
        return lax.rem(z + j % 4, 4) , lax.rem(t + 9 * (j // 4), 16)

    barrier = pltpu.get_barrier_semaphore()

    def greet(j, carry):
        zz, tt = peer64(j)
        pl.semaphore_signal(barrier, inc=1, device_id=(zz * 4 + y, tt), device_id_type=MESH)
        return carry

    lax.fori_loop(1, 64, greet, 0)
    for zz in range(4):
        pl.semaphore_signal(barrier, inc=1, device_id=(zz * 4 + y + 1 - 2 * yi, t), device_id_type=MESH)
    pl.semaphore_signal(barrier, inc=1, device_id=(d_c, t), device_id_type=MESH)

    fetch = [
        pltpu.make_async_copy(src, dst, s_in.at[i])
        for i, (src, dst) in enumerate(
            ((gate_in, gate_ref), (up_in, up_ref), (h256_in, h256_ref), (dw_in, dw_ref), (step_in, step_ref))
        )
    ]
    for copy in fetch:
        copy.start()

    pl.semaphore_wait(barrier, 68)

    def columns(zz, yy, c):
        low = yy - (yy // 2) * (2 * yy - 3)
        return pl.ds(pl.multiple_of(512 * (zz * 4 + low + c * (3 - 2 * low)), 512), 512)

    def send_d1(other):
        yy = y - yi + (yo if other else yi)

        def step(j, carry):
            zz = lax.rem(z + j, 4)
            for c in range(2):
                remote(
                    dy_ref.at[rows16(part), columns(zz, yy, c)],
                    dyb.at[yi, z, rows16(part), pl.ds(512 * c, 512)],
                    s_d1s, s_d1r.at[other], zz * 4 + yy, t,
                ).start()
            return carry

        lax.fori_loop(1 - other, 4, step, 0)

    send_d1(1)
    for c in range(2):
        pltpu.make_async_copy(
            dy_ref.at[rows16(part), columns(z, y, c)],
            dyb.at[yi, z, rows16(part), pl.ds(512 * c, 512)],
            s_d1r.at[0],
        ).start()
    send_d1(0)

    for copy in fetch[:3]:
        copy.wait()

    def hidden_step(i, carry):
        rows = rows16(i)
        for q in range(7):
            cols = slice(256 * q, 256 * q + 256)
            g = gate_ref[rows, cols].astype(F32)
            u = up_ref[rows, cols].astype(F32)
            hid[rows, cols] = (g * jax.nn.sigmoid(g) * u).astype(BF16)
        return carry

    lax.fori_loop(0, 8, hidden_step, 0)
    for q in range(7):
        turned = dot(hid[:, 256 * q : 256 * q + 256], h256_ref[...], 1, 0).astype(BF16)
        hs[0, q] = turned[:, :128]
        hs[1, q] = turned[:, 128:]

    def send_h1(k, carry):
        p = lax.rem(t + 9 * k, 16)
        remote(hs.at[p % 2, :, rows16(p // 2), :], h1.at[pl.ds(7 * t, 7)], s_h1s, s_h1r, d, p).start()
        return carry

    pltpu.make_async_copy(hs.at[lh, :, rows16(tg), :], h1.at[pl.ds(7 * t, 7)], s_h1r).start()
    lax.fori_loop(1, 16, send_h1, 0)

    def quant_group(g, carry):
        step = step_ref[pl.ds(g, 1), :]
        inverse = 1.0 / step

        def chunk(i, inner):
            rows = rows16(g * 16 + i)
            ratios = dw_ref[rows, :].astype(F32) * inverse
            clipped = jnp.clip(ratios, -8.0, 7.0)
            r = clipped - jnp.round(clipped)
            u = r * r
            s = r * horner(sin_series, u)
            c = horner(cos_series, u)
            levels = clipped - s * c * (1.0 / math.pi)
            slope = 2.0 * s * s
            slopes[rows, :] = slope
            extra[rows, :] = levels - ratios * slope
            qb[di, g, rows16(i), :] = (step * levels).astype(BF16)
            return inner

        lax.fori_loop(0, 16, chunk, 0)
        remote(qb.at[di, g], qb.at[di, g], s_qs.at[g], s_qr.at[g], d_c, t).start()
        return carry

    fetch[3].wait()
    fetch[4].wait()
    lax.fori_loop(0, 7, quant_group, 0)

    sibling = t + 1 - 2 * lh

    def d2_block(other, k):
        return dyb.at[yo if other else yi, :, rows16(lax.rem(part + 2 * k, 8)), :]

    def push_d2(other):
        await_bytes(dyb.at[0, :, 0:16, :], s_d1r.at[other])
        block = d2_block(other, 0)

        def send_d2(k, carry):
            remote(block, block, s_d2s, s_d2r.at[other, k], d, hi8 + lax.rem(part + 2 * k, 8)).start()
            return carry

        lax.fori_loop(1, 4, send_d2, 0)
        remote(block, block, s_d3s, s_d3r.at[other], d, sibling).start()

    def push_d3(other):
        def forward_d3(k, carry):
            block = d2_block(other, 4 - k)
            await_bytes(block, s_d2r.at[other, k])
            remote(block, block, s_d3s, s_d3r.at[other], d, sibling).start()
            return carry

        lax.fori_loop(1, 4, forward_d3, 0)

    push_d2(1)
    push_d2(0)
    push_d3(1)

    await_bytes(h1, s_h1r)

    def spread_h(a, carry):
        x = [h1[a * 4 + b].astype(F32) for b in range(4)]
        p0, p1, m0, m1 = x[0] + x[1], x[2] + x[3], x[0] - x[1], x[2] - x[3]
        mixf[0, a] = p0 + p1
        mixf[1, a] = m0 + m1
        mixf[2, a] = p0 - p1
        mixf[3, a] = m0 - m1
        return carry

    lax.fori_loop(0, 28, spread_h, 0)
    mix_paley(paley, mixf, h2, SCALE)

    def h_place(zz, ti):
        return hb.at[yi, ti % 2, :, pl.ds(pl.multiple_of(zz * 128 + (ti // 2) * 16, 16), 16), :]

    def send_h2(j, carry):
        zz, tt = peer64(j)
        remote(h2.at[pl.ds(7 * tt, 7)], h_place(z, t), s_h2s, s_h2r, zz * 4 + y, tt).start()
        return carry

    pltpu.make_async_copy(h2.at[pl.ds(7 * t, 7)], h_place(z, t), s_h2r).start()
    lax.fori_loop(1, 64, send_h2, 0)

    push_d3(0)
    await_bytes(dyb.at[0, :, 0:64, :], s_d3r.at[1])

    def product_g(which, g):
        total = dot(dyb[which, :, :, :512].reshape(512, 512), qb[0, g], 1, 1)
        return total + dot(dyb[which, :, :, 512:].reshape(512, 512), qb[1, g], 1, 1)

    def grad_group(g, carry):
        remote(qb.at[di, g], qb.at[do, g], s_qs.at[g], s_qr.at[g], d_c, t).wait_recv()
        theirs = product_g(yo, g).astype(BF16)
        gsend[g, 0] = theirs[:, :128]
        gsend[g, 1] = theirs[:, 128:]
        remote(gsend.at[g], gx.at[g], s_gxs.at[g], s_gxr.at[g], d_t, t).start()
        return carry

    lax.fori_loop(0, 7, grad_group, 0)
    await_bytes(dyb.at[0, :, 0:64, :], s_d3r.at[0])

    def own_group(g, carry):
        ours = product_g(yi, g).astype(BF16)
        gsum[0, g] = ours[:, :128]
        gsum[1, g] = ours[:, 128:]
        return carry

    lax.fori_loop(0, 7, own_group, 0)

    def factor_step(i, carry):
        rows = rows16(i)
        for q in range(7):
            cols = slice(256 * q, 256 * q + 256)
            g = gate_ref[rows, cols].astype(F32)
            u = up_ref[rows, cols].astype(F32)
            sig = jax.nn.sigmoid(g)
            up_factor[rows, cols] = g * sig
            gate_factor[rows, cols] = u * sig * (1.0 + g * (1.0 - sig))
        return carry

    lax.fori_loop(0, 8, factor_step, 0)

    def add_group(g, carry):
        remote(gsend.at[g], gx.at[g], s_gxs.at[g], s_gxr.at[g], d_t, t).wait_recv()

        def chunk(i, inner):
            rows = pl.ds(pl.multiple_of(i * 64, 64), 64)
            for k in range(2):
                gsum[k, g, rows, :] = (gsum[k, g, rows, :].astype(F32) + gx[g, k, rows, :].astype(F32)).astype(BF16)
            return inner

        return lax.fori_loop(0, 8, chunk, carry)

    def push_g(chunk):
        q0, n = CHUNKS[chunk]

        def piece(zz, ti):
            return gsum.at[ti % 2, q0 : q0 + n, pl.ds(pl.multiple_of(zz * 128 + (ti // 2) * 16, 16), 16), :]

        place = gr.at[pl.ds(z * 112 + 7 * t + q0, n)]

        def send_gr(j, carry):
            zz, tt = peer64(j)
            remote(piece(zz, tt), place, s_grs, s_grr, zz * 4 + y, tt).start()
            return carry

        lax.fori_loop(q0, q0 + n, add_group, 0)
        pltpu.make_async_copy(piece(z, t), place, s_grr).start()
        lax.fori_loop(1, 64, send_gr, 0)

    push_g(0)

    def h_pass(q, which):
        return remote(hb.at[yi, :, q], hb.at[which, :, q], s_hxs.at[q], s_hxr.at[q], d_t, t)

    def forward_h(q, carry):
        h_pass(q, yi).start()
        return carry

    await_bytes(hb.at[yi], s_h2r)
    lax.fori_loop(0, 7, forward_h, 0)
    push_g(1)

    def product_d(q, half, c):
        cols = pl.ds(pl.multiple_of(c * 512, 512), 512)
        total = dot(hb[0, half, q], dyb[0, :, :, cols].reshape(512, 512), 0, 0)
        return total + dot(hb[1, half, q], dyb[1, :, :, cols].reshape(512, 512), 0, 0)

    def weight_group(q, carry):
        h_pass(q, yo).wait_recv()
        for half in range(2):
            dsend[q, 128 * half : 128 * half + 128, :] = product_d(q, half, do).astype(BF16)
        remote(dsend.at[q], dx.at[q], s_xs.at[q], s_xr.at[q], d_c, t).start()
        for half in range(2):
            wg_ref[pl.ds(pl.multiple_of(q * 256 + 128 * half, 128), 128), :] = product_d(q, half, di)
        return carry

    lax.fori_loop(0, 5, weight_group, 0)

    await_bytes(gr, s_grr)

    def spread_g(a, carry):
        x = []
        for b in range(4):
            total = gr[a * 4 + b].astype(F32)
            for zz in range(1, 4):
                total = total + gr[112 * zz + a * 4 + b].astype(F32)
            x.append(total)
        p0, p1, m0, m1 = x[0] + x[1], x[2] + x[3], x[0] - x[1], x[2] - x[3]
        mixf[0, a] = p0 + p1
        mixf[1, a] = m0 + m1
        mixf[2, a] = p0 - p1
        mixf[3, a] = m0 - m1
        return carry

    lax.fori_loop(0, 28, spread_g, 0)
    mix_paley(paley.T, mixf, gm, SCALE)

    def f_place(ti):
        return fr.at[ti % 2, :, rows16(ti // 2), :]

    def send_f(k, carry):
        p = lax.rem(t + 9 * k, 16)
        remote(gm.at[pl.ds(7 * p, 7)], f_place(t), s_fs, s_fr, d, p).start()
        return carry

    pltpu.make_async_copy(gm.at[pl.ds(7 * t, 7)], f_place(t), s_fr).start()
    lax.fori_loop(1, 16, send_f, 0)
    lax.fori_loop(5, 7, weight_group, 0)
    def leave_w(q):
        rows = pl.ds(pl.multiple_of(q * 256, 256), 256)
        return pltpu.make_async_copy(wg_ref.at[rows, :], wg_out.at[rows, :], s_w.at[q])

    def weight_finish(q, carry):
        remote(dsend.at[q], dx.at[q], s_xs.at[q], s_xr.at[q], d_c, t).wait_recv()

        def chunk(i, acc):
            rows = rows16(q * 16 + i)
            total = wg_ref[rows, :] + dx[q, rows16(i), :].astype(F32)
            wg_ref[rows, :] = total * slopes[rows, :]
            return acc + total * extra[rows, :]

        acc = lax.fori_loop(0, 16, chunk, jnp.zeros((16, 512), F32))
        leave_w(q).start()
        sg_ref[pl.ds(q, 1), :] = jnp.sum(acc, axis=0, keepdims=True) * (1.0 / math.sqrt(1792.0))
        return carry

    lax.fori_loop(0, 5, weight_finish, 0)
    await_bytes(fr, s_fr)
    leave_g = []
    for q in range(7):
        gh[...] = dot(fr[0, q], h256_ref[:128, :], 1, 0) + dot(fr[1, q], h256_ref[128:, :], 1, 0)
        cols = slice(256 * q, 256 * q + 256)

        def finish_step(i, carry, cols=cols):
            rows = rows16(i)
            grad = gh[rows, :]
            dup[rows, cols] = (grad * up_factor[rows, cols]).astype(BF16)
            dgate[rows, cols] = (grad * gate_factor[rows, cols]).astype(BF16)
            return carry

        lax.fori_loop(0, 8, finish_step, 0, unroll=True)
        leave_g.append(pltpu.make_async_copy(dgate.at[:, cols], dgate_out.at[:, cols], s_gate.at[q]))
        leave_g.append(pltpu.make_async_copy(dup.at[:, cols], dup_out.at[:, cols], s_up.at[q]))
        leave_g[-1].start()
        leave_g[-2].start()
    lax.fori_loop(5, 7, weight_finish, 0)

    await_bytes(h1.at[0:105], s_h1s)
    await_bytes(gr.at[0:441], s_h2s)
    await_bytes(gr.at[0:441], s_grs)
    await_bytes(gm.at[0:105], s_fs)
    await_bytes(dyb.at[0, 0, 0:112, :], s_d1s)
    await_bytes(dyb.at[:, :, 0:48, :], s_d2s)
    await_bytes(dyb.at[:, :, 0:64, :], s_d3s)

    def drain7(g, carry):
        remote(qb.at[di, g], qb.at[di, g], s_qs.at[g], s_qr.at[g], d_c, t).wait_send()
        remote(gsend.at[g], gx.at[g], s_gxs.at[g], s_gxr.at[g], d_t, t).wait_send()
        remote(dsend.at[g], dx.at[g], s_xs.at[g], s_xr.at[g], d_c, t).wait_send()
        h_pass(g, yi).wait_send()
        leave_w(g).wait()
        return carry

    lax.fori_loop(0, 7, drain7, 0)
    for copy in leave_g:
        copy.wait()


def copy_kernel(dgate_in, dup_in, wg_in, sg_in, dgate_out, dup_out, wg_out, sg_out, dgate, dup, wg, sg, s_in, s_out):
    routes = [(sg_in, sg, sg_out), (dgate_in, dgate, dgate_out), (dup_in, dup, dup_out)]
    for q in range(7):
        rows = pl.ds(256 * q, 256)
        routes.append((wg_in.at[rows, :], wg.at[rows, :], wg_out.at[rows, :]))
    bring = [pltpu.make_async_copy(src, via, s_in.at[i]) for i, (src, via, _) in enumerate(routes)]
    leave = [pltpu.make_async_copy(via, dst, s_out.at[i]) for i, (_, via, dst) in enumerate(routes)]
    for copy in bring:
        copy.start()
    for copy, then in zip(bring, leave):
        copy.wait()
        then.start()
    for copy in leave:
        copy.wait()


def shards(d_out, gate_pre, up_pre, down_weight, step_size):
    h256 = jnp.asarray(sylvester(256), BF16)
    vmem = pl.BlockSpec(memory_space=pltpu.VMEM)
    dma = pltpu.SemaphoreType.DMA
    anywhere = pl.BlockSpec(memory_space=pl.ANY)
    results = pl.pallas_call(
        kernel,
        out_shape=(
            jax.ShapeDtypeStruct((128, 1792), BF16),
            jax.ShapeDtypeStruct((128, 1792), BF16),
            jax.ShapeDtypeStruct((1792, 512), F32),
            jax.ShapeDtypeStruct((7, 512), F32),
        ),
        in_specs=[anywhere] * 6,
        out_specs=(anywhere, anywhere, anywhere, vmem),
        scratch_shapes=[
            pltpu.VMEM((128, 1792), BF16),
            pltpu.VMEM((128, 1792), BF16),
            pltpu.VMEM((1792, 512), BF16),
            pltpu.VMEM((7, 512), F32),
            pltpu.VMEM((256, 256), BF16),
            pltpu.VMEM((128, 1792), BF16),
            pltpu.VMEM((128, 1792), BF16),
            pltpu.VMEM((128, 1792), F32),
            pltpu.VMEM((128, 1792), F32),
            pltpu.VMEM((2, 7, 128, 128), BF16),
            pltpu.VMEM((128, 256), F32),
            pltpu.VMEM((1792, 512), F32),
            pltpu.VMEM((128, 1792), BF16),
            pltpu.VMEM((2, 7, 128, 128), BF16),
            pltpu.VMEM((112, 16, 128), BF16),
            pltpu.VMEM((8, 28, 16, 128), F32),
            pltpu.VMEM((112, 16, 128), BF16),
            pltpu.VMEM((2, 2, 7, 512, 128), BF16),
            pltpu.VMEM((2, 4, 128, 1024), BF16),
            pltpu.VMEM((2, 7, 256, 512), BF16),
            pltpu.VMEM((1792, 512), F32),
            pltpu.VMEM((1792, 512), F32),
            pltpu.VMEM((7, 2, 512, 128), BF16),
            pltpu.VMEM((7, 2, 512, 128), BF16),
            pltpu.VMEM((2, 7, 512, 128), BF16),
            pltpu.VMEM((448, 16, 128), BF16),
            pltpu.VMEM((112, 16, 128), BF16),
            pltpu.VMEM((7, 256, 512), BF16),
            pltpu.VMEM((7, 256, 512), BF16),
            dma, dma,
            dma, dma,
            dma((7,)), dma((7,)),
            dma, dma((2,)),
            dma, dma((2, 4)),
            dma, dma((2,)),
            dma((7,)), dma((7,)),
            dma((7,)), dma((7,)),
            dma, dma,
            dma, dma,
            dma((7,)), dma((7,)),
            dma((7,)),
            dma((5,)), dma((7,)), dma((7,)),
        ],
        compiler_params=pltpu.CompilerParams(
            collective_id=0, has_side_effects=True, vmem_limit_bytes=58 * 1024 * 1024
        ),
        cost_estimate=pl.CostEstimate(flops=8_000_000_000, bytes_accessed=12_000_000, transcendentals=1_000_000),
    )(d_out, gate_pre, up_pre, down_weight, step_size, h256)
    return pl.pallas_call(
        copy_kernel,
        out_shape=(
            jax.ShapeDtypeStruct((128, 1792), BF16),
            jax.ShapeDtypeStruct((128, 1792), BF16),
            jax.ShapeDtypeStruct((1792, 512), F32),
            jax.ShapeDtypeStruct((7, 512), F32),
        ),
        in_specs=[anywhere] * 4,
        out_specs=(anywhere,) * 4,
        scratch_shapes=[
            pltpu.VMEM((128, 1792), BF16),
            pltpu.VMEM((128, 1792), BF16),
            pltpu.VMEM((1792, 512), F32),
            pltpu.VMEM((7, 512), F32),
            dma((10,)), dma((10,)),
        ],
        compiler_params=pltpu.CompilerParams(vmem_limit_bytes=60 * 1024 * 1024),
        cost_estimate=pl.CostEstimate(flops=0, bytes_accessed=10_000_000, transcendentals=0),
    )(*results)


def solution(mesh):
    return jax.shard_map(
        shards,
        mesh=mesh,
        in_specs=(
            P("dp", None),
            P("dp", "tensor"),
            P("dp", "tensor"),
            P("tensor", "dp"),
            P("tensor", "dp"),
        ),
        out_specs=(P("dp", "tensor"), P("dp", "tensor"), P("tensor", "dp"), P("tensor", "dp")),
        check_vma=False,
    )
```
